512 devices in a mesh: pitch: 64 (over x, y, z_hi), radial: 8 (over z_lo, core).
Axes of the slice: x: 4, y: 8, z: 8 (z_hi: 2, z_lo: 4; z = z_hi * 4 + z_lo), core: 2. Of those that a mesh axis runs over, the one named last changes fastest.
Arguments:
- vel: float32 [3, 512, 64, 256], P(None, 'pitch', 'radial'), may hold values from -6 to 6
- rhs_mom: float32 [3, 512, 64, 256], P(None, 'pitch', 'radial'), may hold values from -6 to 6
- mode_inv: float32 [512, 64, 8], P(None, 'radial'), may hold values from -0.4 to 2
- sweep_inv: float32 [3, 3, 512, 64, 256], P(None, None, 'pitch', 'radial'), may hold values from -0.07 to 0.25
Outputs:
- velocity: float32 [3, 512, 64, 256], P(None, 'pitch', 'radial')
- pressure: float32 [512, 64, 256], P('pitch', 'radial')
The draws below stay inside these ranges and needn't reach their ends.
All inputs are finite; a program needn't handle non-finite values.
Results may differ from the reference program's by a relative error of at most 0.00007.
Values sent between devices are 32-bit elements; how exact they have to be, the bound alone decides.
No kernel may reach another device: no remote copies, remote signals or barrier semaphores. Data moves between devices by JAX's collectives and lax.ppermute only.
A program may use at most 64 MiB of HBM per device.

```python
import jax
import jax.numpy as jnp
from jax import lax

CR = 8
SWEEPS = 4
NP = 512
NR = 64
NZ = 256
N_RADIAL = 8


def draw_mode_inv(key, part):
    key = jax.random.fold_in(key, 11)
    diag_key, off_key = jax.random.split(key)
    diag_vals = jax.random.uniform(diag_key, (NP, NR, CR), jnp.float32, 0.5, 2.0)
    off_vals = jax.random.uniform(off_key, (NP, NR, CR), jnp.float32, -0.4, 0.4)
    rows = jnp.arange(NR, dtype=jnp.int32)
    cols = jnp.arange(CR, dtype=jnp.int32)
    on_diag = rows[:, None] % CR == cols[None, :]
    return jnp.where(on_diag[None, :, :], diag_vals, off_vals)


def draw_sweep_inv(key, part):
    key = jax.random.fold_in(key, 23)
    diag_key, off_key = jax.random.split(key)
    diag_vals = jax.random.uniform(diag_key, (3, 3, NP, NR, NZ), jnp.float32, 0.45, 1.0) * 0.25
    off_vals = jax.random.uniform(off_key, (3, 3, NP, NR, NZ), jnp.float32, -0.07, 0.07)
    comps = jnp.arange(3, dtype=jnp.int32)
    on_diag = comps[:, None] == comps[None, :]
    return jnp.where(on_diag[:, :, None, None, None], diag_vals, off_vals)


def level_of(stream_key, dims, pieces, smallest, high):
    loudness = 1.0
    for dim, shards_of in pieces:
        steps = jax.random.uniform(jax.random.fold_in(jax.random.fold_in(stream_key, 6), dim), (shards_of,), jnp.float32, smallest / len(pieces), high / len(pieces))
        loudness = loudness * jnp.repeat(jnp.exp(steps), dims[dim] // shards_of).reshape((-1,) + (1,) * (len(dims) - 1 - dim))
    return loudness


def noise(key, extent, spread, most, pieces=(), kind=jnp.bfloat16):
    result = spread * jax.random.normal(key, extent, jnp.float32)
    if pieces:
        result = result * level_of(key, extent, pieces, -0.22, 0.18)
    return jnp.clip(result, -most, most).astype(kind)


def setup_inputs(seed: int = 0) -> dict:
    arg_keys = jax.random.split(jax.random.key(seed), 5)
    vel = noise(arg_keys[0], (3, NP, NR, NZ), 1.0, 6.0, ((1, 64), (2, 8)), jnp.float32)
    rhs_mom = noise(arg_keys[1], (3, NP, NR, NZ), 1.0, 6.0, ((1, 64), (2, 8)), jnp.float32)
    mode_inv = draw_mode_inv(jax.random.fold_in(arg_keys[4], 71), 0)
    sweep_inv = draw_sweep_inv(jax.random.fold_in(arg_keys[4], 71), 0)
    return dict(vel=vel, rhs_mom=rhs_mom, mode_inv=mode_inv, sweep_inv=sweep_inv)


coupling = 0.5


def cas_table(count):
    index = jnp.arange(count, dtype=jnp.int32)
    product = (index[:, None] * index[None, :]) % count
    angle = (2.0 * jnp.pi / count) * product.astype(jnp.float32)
    return jnp.cos(angle) + jnp.sin(angle)


def central(field, axis, periodic):
    if periodic:
        return (jnp.roll(field, -1, axis) - jnp.roll(field, 1, axis)) * 0.5
    padded = jnp.pad(field, [(1, 1) if a == axis else (0, 0) for a in range(field.ndim)])
    upper = lax.slice_in_dim(padded, 2, padded.shape[axis], axis=axis)
    lower = lax.slice_in_dim(padded, 0, padded.shape[axis] - 2, axis=axis)
    return (upper - lower) * 0.5


def neighbours(field, axis, periodic):
    if periodic:
        return jnp.roll(field, -1, axis) + jnp.roll(field, 1, axis)
    padded = jnp.pad(field, [(1, 1) if a == axis else (0, 0) for a in range(field.ndim)])
    upper = lax.slice_in_dim(padded, 2, padded.shape[axis], axis=axis)
    lower = lax.slice_in_dim(padded, 0, padded.shape[axis] - 2, axis=axis)
    return upper + lower


def reference(vel, rhs_mom, mode_inv, sweep_inv):
    highest = lax.Precision.HIGHEST
    div = central(vel[0], 0, True) + central(vel[1], 1, False) + central(vel[2], 2, False)
    table = cas_table(NP)
    dhat = jnp.dot(table, div.reshape(NP, -1), precision=highest).reshape(NP, N_RADIAL, CR, NZ)
    blocks = mode_inv.reshape(NP, N_RADIAL, CR, CR)
    modes = jnp.einsum("kbrs,kbsz->kbrz", blocks, dhat, precision=highest)
    pressure = jnp.dot(table, modes.reshape(NP, -1), precision=highest).reshape(NP, NR, NZ) / NP
    grads = jnp.stack([central(pressure, 0, True), central(pressure, 1, False), central(pressure, 2, False)])
    force = rhs_mom - grads
    state = vel
    for sweep in range(SWEEPS):
        beside_all = neighbours(state, 1, True) + neighbours(state, 2, False) + neighbours(state, 3, False)
        res = force - ((1.0 + 6.0 * coupling) * state - coupling * beside_all)
        state = state + sweep_inv[:, 0] * res[0] + sweep_inv[:, 1] * res[1] + sweep_inv[:, 2] * res[2]
    return state, pressure
```

```python
import jax
import jax.numpy as jnp
import ml_dtypes
import numpy as np
from jax import lax
from jax.experimental import pallas as pl
from jax.experimental.pallas import tpu as pltpu
from jax.sharding import PartitionSpec as P

SWEEPS = 4
coupling = 0.5
NP, CR, NZ = 512, 8, 256
BLOCKS = 64
LINES = NP // BLOCKS
CHUNK = NZ // BLOCKS
F32 = jnp.float32
BF16 = jnp.bfloat16


def cas_tables():
    index = np.arange(NP)
    angle = 2.0 * np.pi / NP * (index[:, None] * index[None, :] % NP)
    table = np.cos(angle) + np.sin(angle)
    order = (np.arange(BLOCKS)[None, :] * LINES + np.arange(LINES)[:, None]).reshape(-1)
    out = []
    for mat in (table[order, :], table[:, order] / NP):
        high = mat.astype(ml_dtypes.bfloat16)
        low = (mat - high.astype(np.float64)).astype(ml_dtypes.bfloat16)
        out += [high, low]
    return out


def params(mib=24):
    return pltpu.CompilerParams(vmem_limit_bytes=mib * 1024 * 1024)


VMEM = pl.BlockSpec(memory_space=pltpu.VMEM)


def shape(*dims):
    return jax.ShapeDtypeStruct(dims, F32)


def axial(x, step):
    lane = lax.broadcasted_iota(jnp.int32, x.shape, x.ndim - 1)
    moved = pltpu.roll(x, (-step) % NZ, x.ndim - 1)
    return jnp.where(lane == (NZ - 1 if step > 0 else 0), 0.0, moved)


def face_kernel(v1, up, down):
    up[...] = v1[0, :, CR - 1, :]
    down[...] = v1[0, :, 0, :]


def div_kernel(vel, low, high, out):
    row = lax.broadcasted_iota(jnp.int32, (CR, NZ), 0)
    parts = []
    for l in range(LINES):
        v1, v2 = vel[1, l], vel[2, l]
        upper = jnp.where(row == CR - 1, high[l : l + 1, :], pltpu.roll(v1, CR - 1, 0))
        lower = jnp.where(row == 0, low[l : l + 1, :], pltpu.roll(v1, 1, 0))
        parts.append(((upper - lower) + (axial(v2, 1) - axial(v2, -1))) * 0.5)
    for l in range(LINES):
        parts.append(vel[0, l])
    out[...] = jnp.concatenate(parts, axis=0).T


def block_shift(x, step):
    lane = lax.broadcasted_iota(jnp.int32, x.shape, 1) % BLOCKS
    edge = BLOCKS - 1 if step > 0 else 0
    near = pltpu.roll(x, (-step) % 128, 1)
    far = pltpu.roll(x, (BLOCKS - step) % 128, 1)
    return jnp.where(lane == edge, far, near)


def split_dot(x, high, low):
    xh = x.astype(BF16)
    xl = (x - xh.astype(F32)).astype(BF16)
    rows = x.shape[0]
    both = jnp.dot(jnp.concatenate([xh, xl], axis=0), high[...], preferred_element_type=F32)
    return both[:rows] + (both[rows:] + jnp.dot(xh, low[...], preferred_element_type=F32))


def modes_kernel(got, mode, h1, l1, h2, l2, out):
    lane = lax.broadcasted_iota(jnp.int32, (CR, 128), 1)
    sub = lax.broadcasted_iota(jnp.int32, (CR, 128), 0)
    left = lane < BLOCKS
    half = CHUNK // 2
    rows = [[None] * 4 for _ in range(CHUNK)]
    for pair in range(half):
        slabs = [got[pl.ds(2 * pair + e, BLOCKS, stride=CHUNK), :] for e in range(2)]
        a = jnp.concatenate(slabs, axis=0).T
        w = [a[l * CR : (l + 1) * CR] for l in range(LINES)]
        v = [a[NP // 8 + l * CR : NP // 8 + (l + 1) * CR] for l in range(LINES)]
        before = [block_shift(v[-1], -1)] + v[:-1]
        after = v[1:] + [block_shift(v[0], 1)]
        d = [w[l] + (after[l] - before[l]) * 0.5 for l in range(LINES)]
        for t in range(4):
            e, o = d[2 * t], d[2 * t + 1]
            rows[2 * pair][t] = jnp.where(left, e, pltpu.roll(o, BLOCKS, 1))
            rows[2 * pair + 1][t] = jnp.where(left, pltpu.roll(e, BLOCKS, 1), o)
    x = jnp.concatenate([jnp.concatenate(r, axis=1) for r in rows], axis=0)
    dhat = split_dot(x, h1, l1)
    q = []
    for z in range(CHUNK):
        total = None
        for s in range(CR):
            term = mode[:, s, :] * dhat[z * CR + s : z * CR + s + 1, :]
            total = term if total is None else total + term
        q.append(total)
    p = split_dot(jnp.concatenate(q, axis=0), h2, l2)
    for pair in range(half):
        e = []
        for t in range(4):
            a = p[2 * pair * CR : (2 * pair + 1) * CR, t * 128 : (t + 1) * 128]
            b = p[(2 * pair + 1) * CR : (2 * pair + 2) * CR, t * 128 : (t + 1) * 128]
            e.append(jnp.where(left, a, pltpu.roll(b, BLOCKS, 1)))
            e.append(jnp.where(left, pltpu.roll(a, BLOCKS, 1), b))
        wide = [block_shift(x, -1) for x in e[4:]] + e + [block_shift(x, 1) for x in e[:4]]
        low, high = [], []
        for m in range(8):
            a, b = wide[2 * m], wide[2 * m + 1]
            low.append(jnp.where(sub < 4, a, pltpu.roll(b, 4, 0)))
            high.append(jnp.where(sub < 4, pltpu.roll(a, 4, 0), b))
        turned = jnp.concatenate(low + high, axis=0).T
        for z in range(2):
            out[pl.ds(2 * pair + z, BLOCKS, stride=CHUNK), :] = turned[
                z * BLOCKS : (z + 1) * BLOCKS
            ]


def pack_kernel(vel, rhs, inv, fwd, bwd, up, down):
    for c in range(3):
        for d in range(3):
            f = 3 * c + d
            fwd[3 * f : 3 * f + 3] = inv[c, d, 5:8]
            bwd[3 * f : 3 * f + 3] = inv[c, d, 0:3]
            up[f] = inv[c, d, :, 4:8, :]
            down[f] = inv[c, d, :, 0:4, :]
        fwd[27 + 3 * c : 30 + 3 * c] = rhs[c, 5:8]
        bwd[27 + 3 * c : 30 + 3 * c] = rhs[c, 0:3]
        up[9 + c] = rhs[c, :, 4:8, :]
        down[9 + c] = rhs[c, :, 0:4, :]
        fwd[36 + 4 * c : 40 + 4 * c] = vel[c, 4:8]
        bwd[36 + 4 * c : 40 + 4 * c] = vel[c, 0:4]
        up[12 + c] = vel[c, :, 4:8, :]
        down[12 + c] = vel[c, :, 0:4, :]


def corner_kernel(got, before, after, press, up, down):
    turned = got[...].T
    press[...] = turned
    for out, first, part in ((up, 4, 64), (down, 0, 0)):
        two = first + 2 if first else 0
        for m in range(8):
            out[m] = turned[part + 8 * m : part + 8 * m + 8]
        for f in range(12):
            for n, src in enumerate((before[3 * f + 1], before[3 * f + 2], after[3 * f], after[3 * f + 1])):
                out[8 + f, 2 * n : 2 * n + 2, :] = src[two : two + 2]
        for c in range(3):
            g = 36 + 4 * c
            out[20 + 2 * c, 0:4, :] = before[g + 3, first : first + 4, :]
            out[20 + 2 * c, 4:8, :] = after[g, first : first + 4, :]
            for n, src in enumerate((before[g + 1], before[g + 2], after[g + 1], after[g + 2])):
                out[21 + 2 * c, 2 * n : 2 * n + 2, :] = src[two : two + 2]


def sweep_kernel(vel, rhs, inv, press, before, after, rad_low, rad_high, cor_low, cor_high,
                 velocity, pressure, es, ef, eu, ep):
    for l in range(16):
        ep[l, 4:8, :] = press[4 * l : 4 * l + 4]
        ep[l, 8:12, :] = press[64 + 4 * l : 68 + 4 * l]
        ep[l, 0:4, :] = cor_low[l // 2, 4 * (l % 2) : 4 * (l % 2) + 4, :]
        ep[l, 12:16, :] = cor_high[l // 2, 4 * (l % 2) : 4 * (l % 2) + 4, :]
    for l in range(LINES):
        pressure[l] = ep[l + 4, 4:12, :]
    for f in range(12):
        c, d = f // 3, f % 3
        dst = es.at[f] if f < 9 else ef.at[f - 9]
        own = inv.at[c, d] if f < 9 else rhs.at[f - 9]
        dst[3:11, 4:12, :] = own[...]
        dst[3:11, 0:4, :] = rad_low[f]
        dst[3:11, 12:16, :] = rad_high[f]
        dst[0:3, 4:12, :] = before[3 * f : 3 * f + 3]
        dst[11:14, 4:12, :] = after[3 * f : 3 * f + 3]
        for n, line in enumerate((1, 2, 11, 12)):
            dst[line, 2:4, :] = cor_low[8 + f, 2 * n : 2 * n + 2, :]
            dst[line, 12:14, :] = cor_high[8 + f, 2 * n : 2 * n + 2, :]
    for c in range(3):
        dst = eu.at[0, c]
        g = 36 + 4 * c
        dst[4:12, 4:12, :] = vel[c]
        dst[4:12, 0:4, :] = rad_low[12 + c]
        dst[4:12, 12:16, :] = rad_high[12 + c]
        dst[0:4, 4:12, :] = before[g : g + 4]
        dst[12:16, 4:12, :] = after[g : g + 4]
        for n, line in enumerate((3, 12)):
            dst[line, 0:4, :] = cor_low[20 + 2 * c, 4 * n : 4 * n + 4, :]
            dst[line, 12:16, :] = cor_high[20 + 2 * c, 4 * n : 4 * n + 4, :]
        for n, line in enumerate((1, 2, 13, 14)):
            dst[line, 2:4, :] = cor_low[21 + 2 * c, 2 * n : 2 * n + 2, :]
            dst[line, 12:14, :] = cor_high[21 + 2 * c, 2 * n : 2 * n + 2, :]

    def line_step(sweep, j):
        now, later = sweep % 2, 1 - sweep % 2
        if sweep == 0:
            mid = ep[j + 1]
            ef[0, j] = ef[0, j] - (ep[j + 2] - ep[j]) * 0.5
            ef[1, j] = ef[1, j] - (pltpu.roll(mid, 15, 0) - pltpu.roll(mid, 1, 0)) * 0.5
            ef[2, j] = ef[2, j] - (axial(mid, 1) - axial(mid, -1)) * 0.5
        state, res = [], []
        for c in range(3):
            u = eu[now, c, j + 1]
            beside = (eu[now, c, j] + eu[now, c, j + 2]) + (pltpu.roll(u, 15, 0) + pltpu.roll(u, 1, 0))
            beside = beside + (axial(u, 1) + axial(u, -1))
            state.append(u)
            res.append(ef[c, j] - ((1.0 + 6.0 * coupling) * u - coupling * beside))
        for c in range(3):
            new = state[c] + es[3 * c, j] * res[0] + es[3 * c + 1, j] * res[1] + es[3 * c + 2, j] * res[2]
            if sweep == SWEEPS - 1:
                velocity[c, j - 3] = new[4:12]
            else:
                eu[later, c, j + 1] = new

    for sweep in range(SWEEPS):
        @pl.loop(sweep, 14 - sweep)
        def _(j, sweep=sweep):
            line_step(sweep, j)


def both_ways(up, down, axis, periodic):
    count = lax.axis_size(axis)
    forward = [(i, i + 1) for i in range(count - 1)]
    if periodic:
        forward.append((count - 1, 0))
    backward = [(target, source) for source, target in forward]
    return lax.ppermute(up, axis, forward), lax.ppermute(down, axis, backward)


def on_device(vel, rhs_mom, mode_inv, sweep_inv):
    h1, l1, h2, l2 = [jnp.asarray(t) for t in cas_tables()]
    up, down = pl.pallas_call(
        face_kernel,
        grid=(1,),
        in_specs=[pl.BlockSpec((1, LINES, CR, NZ), lambda i: (1, 0, 0, 0))],
        out_specs=[pl.BlockSpec((LINES, NZ), lambda i: (0, 0))] * 2,
        out_shape=[shape(LINES, NZ)] * 2,
        compiler_params=params(),
        name="faces",
    )(vel)
    low, high = both_ways(up, down, "radial", False)
    sent = pl.pallas_call(
        div_kernel,
        in_specs=[VMEM] * 3,
        out_specs=VMEM,
        out_shape=shape(NZ, 128),
        compiler_params=params(),
        name="divergence",
    )(vel, low, high)
    sent = sent.reshape(BLOCKS, CHUNK, 128)
    got = lax.all_to_all(sent, "pitch", split_axis=0, concat_axis=0, tiled=True)

    vel_b, rhs_b, inv_b, _ = lax.optimization_barrier((vel, rhs_mom, sweep_inv, sent))
    fwd, bwd, up, down = pl.pallas_call(
        pack_kernel,
        in_specs=[VMEM] * 3,
        out_specs=[VMEM] * 4,
        out_shape=[shape(48, CR, NZ)] * 2 + [shape(15, LINES, 4, NZ)] * 2,
        compiler_params=params(),
        name="pack",
    )(vel_b, rhs_b, inv_b)
    before, after = both_ways(fwd, bwd, "pitch", True)

    modes = jnp.transpose(mode_inv, (1, 2, 0))
    sent = pl.pallas_call(
        modes_kernel,
        in_specs=[VMEM] * 6,
        out_specs=VMEM,
        out_shape=shape(NZ, 128),
        compiler_params=params(),
        name="modes",
    )(got.reshape(NZ, 128), modes, h1, l1, h2, l2)
    sent = sent.reshape(BLOCKS, CHUNK, 128)
    got = lax.all_to_all(sent, "pitch", split_axis=0, concat_axis=0, tiled=True)
    up, down, _ = lax.optimization_barrier((up, down, sent))
    rad_low, rad_high = both_ways(up, down, "radial", False)

    press, up, down = pl.pallas_call(
        corner_kernel,
        in_specs=[VMEM] * 3,
        out_specs=[VMEM] * 3,
        out_shape=[shape(128, NZ)] + [shape(26, CR, NZ)] * 2,
        compiler_params=params(),
        name="corners",
    )(got.reshape(NZ, 128), before, after)
    cor_low, cor_high = both_ways(up, down, "radial", False)

    return pl.pallas_call(
        sweep_kernel,
        in_specs=[VMEM] * 10,
        out_specs=[VMEM] * 2,
        out_shape=[shape(3, LINES, CR, NZ), shape(LINES, CR, NZ)],
        scratch_shapes=[
            pltpu.VMEM((9, 14, 16, NZ), F32),
            pltpu.VMEM((3, 14, 16, NZ), F32),
            pltpu.VMEM((2, 3, 16, 16, NZ), F32),
            pltpu.VMEM((16, 16, NZ), F32),
        ],
        compiler_params=params(),
        name="sweeps",
    )(vel, rhs_mom, sweep_inv, press, before, after, rad_low, rad_high, cor_low, cor_high)


def solution(mesh):
    return jax.shard_map(
        on_device,
        mesh=mesh,
        in_specs=(
            P(None, "pitch", "radial", None),
            P(None, "pitch", "radial", None),
            P(None, "radial", None),
            P(None, None, "pitch", "radial", None),
        ),
        out_specs=(P(None, "pitch", "radial", None), P("pitch", "radial", None)),
        check_vma=False,
    )
```

```python
import functools

import jax
import jax.numpy as jnp
import ml_dtypes
import numpy as np
from jax import lax
from jax.experimental import pallas as pl
from jax.experimental.pallas import tpu as pltpu
from jax.sharding import PartitionSpec as P

SWEEPS = 4
FIRST = (13,)
BULK = tuple(range(13)) + (14,)
coupling = 0.5
NP, CR, NZ = 512, 8, 256
BLOCKS = 64
LINES = NP // BLOCKS
CHUNK = NZ // BLOCKS
F32 = jnp.float32
BF16 = jnp.bfloat16


def cas_tables():
    index = np.arange(NP)
    angle = 2.0 * np.pi / NP * (index[:, None] * index[None, :] % NP)
    table = np.cos(angle) + np.sin(angle)
    order = (np.arange(BLOCKS)[None, :] * LINES + np.arange(LINES)[:, None]).reshape(-1)
    mat = table[order, :]
    high = mat.astype(ml_dtypes.bfloat16)
    low = (mat - high.astype(np.float64)).astype(ml_dtypes.bfloat16)
    return np.concatenate([high, low])


def params(mib=24):
    return pltpu.CompilerParams(vmem_limit_bytes=mib * 1024 * 1024)


VMEM = pl.BlockSpec(memory_space=pltpu.VMEM)


def shape(*dims):
    return jax.ShapeDtypeStruct(dims, F32)


def axial(x, step):
    lane = lax.broadcasted_iota(jnp.int32, x.shape, x.ndim - 1)
    moved = pltpu.roll(x, (-step) % NZ, x.ndim - 1)
    return jnp.where(lane == (NZ - 1 if step > 0 else 0), 0.0, moved)


def rows_of(vel, rhs, inv, f):
    return inv.at[f // 3, f % 3] if f < 9 else rhs.at[f - 9] if f < 12 else vel.at[f - 12]


def pack_rows(fields, vel, rhs, inv, up, down):
    for n, f in enumerate(fields):
        src = rows_of(vel, rhs, inv, f)
        up[n] = src[:, 4:8, :]
        down[n] = src[:, 0:4, :]


def div_kernel(vel, low, high, out):
    row = lax.broadcasted_iota(jnp.int32, (CR, NZ), 0)
    parts = []
    for l in range(LINES):
        v1, v2 = vel[1, l], vel[2, l]
        upper = jnp.where(row == CR - 1, high[0, l, 0:1, :], pltpu.roll(v1, CR - 1, 0))
        lower = jnp.where(row == 0, low[0, l, 3:4, :], pltpu.roll(v1, 1, 0))
        parts.append(((upper - lower) + (axial(v2, 1) - axial(v2, -1))) * 0.5)
    for l in range(LINES):
        parts.append(vel[0, l])
    out[...] = jnp.concatenate(parts, axis=0).T


def block_shift(x, step):
    lane = lax.broadcasted_iota(jnp.int32, x.shape, 1) % BLOCKS
    edge = BLOCKS - 1 if step > 0 else 0
    near = pltpu.roll(x, (-step) % 128, 1)
    far = pltpu.roll(x, (BLOCKS - step) % 128, 1)
    return jnp.where(lane == edge, far, near)


def split_dot(x, table, dim):
    dims = (((1,), (dim,)), ((), ()))
    xh = x.astype(BF16)
    xl = (x - xh.astype(F32)).astype(BF16)
    rows = x.shape[0]
    both = jnp.concatenate([xh, xl], axis=0)
    both = lax.dot_general(both, table[0:NP], dims, preferred_element_type=F32)
    cross = lax.dot_general(xh, table[NP : 2 * NP], dims, preferred_element_type=F32)
    return both[:rows] + (both[rows:] + cross)


def modes_kernel(got, mode, table, out):
    lane = lax.broadcasted_iota(jnp.int32, (CR, 128), 1)
    sub = lax.broadcasted_iota(jnp.int32, (CR, 128), 0)
    left = lane < BLOCKS
    half = CHUNK // 2
    rows = [[None] * 4 for _ in range(CHUNK)]
    for pair in range(half):
        slabs = [got[pl.ds(2 * pair + e, BLOCKS, stride=CHUNK), :] for e in range(2)]
        a = jnp.concatenate(slabs, axis=0).T
        w = [a[l * CR : (l + 1) * CR] for l in range(LINES)]
        v = [a[NP // 8 + l * CR : NP // 8 + (l + 1) * CR] for l in range(LINES)]
        before = [block_shift(v[-1], -1)] + v[:-1]
        after = v[1:] + [block_shift(v[0], 1)]
        d = [w[l] + (after[l] - before[l]) * 0.5 for l in range(LINES)]
        for t in range(4):
            e, o = d[2 * t], d[2 * t + 1]
            rows[2 * pair][t] = jnp.where(left, e, pltpu.roll(o, BLOCKS, 1))
            rows[2 * pair + 1][t] = jnp.where(left, pltpu.roll(e, BLOCKS, 1), o)
    x = jnp.concatenate([jnp.concatenate(r, axis=1) for r in rows], axis=0)
    dhat = split_dot(x, table, 0)
    q = []
    for z in range(CHUNK):
        total = None
        for s in range(CR):
            term = mode[:, s, :] * dhat[z * CR + s : z * CR + s + 1, :]
            total = term if total is None else total + term
        q.append(total)
    p = split_dot(jnp.concatenate(q, axis=0), table, 1) * (1.0 / NP)
    for pair in range(half):
        e = []
        for t in range(4):
            a = p[2 * pair * CR : (2 * pair + 1) * CR, t * 128 : (t + 1) * 128]
            b = p[(2 * pair + 1) * CR : (2 * pair + 2) * CR, t * 128 : (t + 1) * 128]
            e.append(jnp.where(left, a, pltpu.roll(b, BLOCKS, 1)))
            e.append(jnp.where(left, pltpu.roll(a, BLOCKS, 1), b))
        wide = [block_shift(x, -1) for x in e[4:]] + e + [block_shift(x, 1) for x in e[:4]]
        low, high = [], []
        for m in range(8):
            a, b = wide[2 * m], wide[2 * m + 1]
            low.append(jnp.where(sub < 4, a, pltpu.roll(b, 4, 0)))
            high.append(jnp.where(sub < 4, pltpu.roll(a, 4, 0), b))
        turned = jnp.concatenate(low + high, axis=0).T
        for z in range(2):
            out[pl.ds(2 * pair + z, BLOCKS, stride=CHUNK), :] = turned[
                z * BLOCKS : (z + 1) * BLOCKS
            ]


def pack_forward(vel, rhs, inv, fwd):
    for f in range(9):
        fwd[3 * f : 3 * f + 3] = inv[f // 3, f % 3, 1:4]
    for c in range(3):
        fwd[27 + 3 * c : 30 + 3 * c] = rhs[c, 1:4]
        fwd[36 + 4 * c : 40 + 4 * c] = vel[c]


def pack_rest(vel, rhs, inv, bwd, up, down):
    for f in range(9):
        bwd[3 * f : 3 * f + 3] = inv[f // 3, f % 3, 0:3]
    for c in range(3):
        bwd[27 + 3 * c : 30 + 3 * c] = rhs[c, 0:3]
        bwd[36 + 4 * c : 40 + 4 * c] = vel[c, 0:4]
    pack_rows(BULK, vel, rhs, inv, up, down)


def corner_kernel(side, halo, up, down):
    for out, first in ((up, 4), (down, 0)):
        two = first + 2 if first else 0
        for f in range(12):
            for n in range(2):
                src = halo[3 * f + n + 1 - side]
                out[f // 2, 4 * (f % 2) + 2 * n : 4 * (f % 2) + 2 * n + 2, :] = src[two : two + 2]
        for c in range(3):
            g = 36 + 4 * c
            out[6 + c, 0:4, :] = halo[g + 3 - 3 * side, first : first + 4, :]
            for n in range(2):
                src = halo[g + 1 + n]
                out[6 + c, 4 + 2 * n : 6 + 2 * n, :] = src[two : two + 2]


def turn_kernel(got, bef_up, bef_down, aft_up, aft_down, press, up, down):
    turned = got[...].T
    press[...] = turned
    for m in range(8):
        up[m] = turned[64 + 8 * m : 72 + 8 * m]
        down[m] = turned[8 * m : 8 * m + 8]
    up[8:17] = bef_up[...]
    down[8:17] = bef_down[...]
    up[17:26] = aft_up[...]
    down[17:26] = aft_down[...]


def beyond(f, first, bulk):
    return first[FIRST.index(f)] if f in FIRST else bulk[BULK.index(f)]


def sweep_kernel(vel, rhs, inv, press, before, after, low, high, rad_low, rad_high, cor_low, cor_high,
                 velocity, pressure, es, ef, eu, ep):
    for l in range(16):
        ep[l, 4:8, :] = press[4 * l : 4 * l + 4]
        ep[l, 8:12, :] = press[64 + 4 * l : 68 + 4 * l]
        ep[l, 0:4, :] = cor_low[l // 2, 4 * (l % 2) : 4 * (l % 2) + 4, :]
        ep[l, 12:16, :] = cor_high[l // 2, 4 * (l % 2) : 4 * (l % 2) + 4, :]
    for l in range(LINES):
        pressure[l] = ep[l + 4, 4:12, :]
    for f in range(12):
        c, d = f // 3, f % 3
        dst = es.at[f] if f < 9 else ef.at[f - 9]
        own = inv.at[c, d] if f < 9 else rhs.at[f - 9]
        dst[3:11, 4:12, :] = own[...]
        dst[3:11, 0:4, :] = beyond(f, low, rad_low)
        dst[3:11, 12:16, :] = beyond(f, high, rad_high)
        dst[0:3, 4:12, :] = before[3 * f : 3 * f + 3]
        dst[11:14, 4:12, :] = after[3 * f : 3 * f + 3]
        for n, line in enumerate((1, 2, 11, 12)):
            t, r = 8 + 9 * (n // 2) + f // 2, 4 * (f % 2) + 2 * (n % 2)
            dst[line, 2:4, :] = cor_low[t, r : r + 2, :]
            dst[line, 12:14, :] = cor_high[t, r : r + 2, :]
    for c in range(3):
        dst = eu.at[0, c]
        g = 36 + 4 * c
        dst[4:12, 4:12, :] = vel[c]
        dst[4:12, 0:4, :] = beyond(12 + c, low, rad_low)
        dst[4:12, 12:16, :] = beyond(12 + c, high, rad_high)
        dst[0:4, 4:12, :] = before[g : g + 4]
        dst[12:16, 4:12, :] = after[g : g + 4]
        for n, line in enumerate((3, 12)):
            t = 14 + 9 * n + c
            dst[line, 0:4, :] = cor_low[t, 0:4, :]
            dst[line, 12:16, :] = cor_high[t, 0:4, :]
        for n, line in enumerate((1, 2, 13, 14)):
            t, r = 14 + 9 * (n // 2) + c, 4 + 2 * (n % 2)
            dst[line, 2:4, :] = cor_low[t, r : r + 2, :]
            dst[line, 12:14, :] = cor_high[t, r : r + 2, :]

    def line_step(sweep, j):
        now, later = sweep % 2, 1 - sweep % 2
        if sweep == 0:
            mid = ep[j + 1]
            ef[0, j] = ef[0, j] - (ep[j + 2] - ep[j]) * 0.5
            ef[1, j] = ef[1, j] - (pltpu.roll(mid, 15, 0) - pltpu.roll(mid, 1, 0)) * 0.5
            ef[2, j] = ef[2, j] - (axial(mid, 1) - axial(mid, -1)) * 0.5
        state, res = [], []
        for c in range(3):
            u = eu[now, c, j + 1]
            beside = (eu[now, c, j] + eu[now, c, j + 2]) + (pltpu.roll(u, 15, 0) + pltpu.roll(u, 1, 0))
            beside = beside + (axial(u, 1) + axial(u, -1))
            state.append(u)
            res.append(ef[c, j] - ((1.0 + 6.0 * coupling) * u - coupling * beside))
        for c in range(3):
            new = state[c] + es[3 * c, j] * res[0] + es[3 * c + 1, j] * res[1] + es[3 * c + 2, j] * res[2]
            if sweep == SWEEPS - 1:
                velocity[c, j - 3] = new[4:12]
            else:
                eu[later, c, j + 1] = new

    for sweep in range(SWEEPS):
        @pl.loop(sweep, 14 - sweep)
        def _(j, sweep=sweep):
            line_step(sweep, j)


def both_ways(up, down, axis, periodic):
    count = lax.axis_size(axis)
    forward = [(i, i + 1) for i in range(count - 1)]
    if periodic:
        forward.append((count - 1, 0))
    backward = [(target, source) for source, target in forward]
    return lax.ppermute(up, axis, forward), lax.ppermute(down, axis, backward)


def corners(side, halo):
    return pl.pallas_call(
        functools.partial(corner_kernel, side),
        in_specs=[VMEM],
        out_specs=[VMEM] * 2,
        out_shape=[shape(9, CR, NZ)] * 2,
        compiler_params=params(8),
        name="corners",
    )(halo)


def on_device(vel, rhs_mom, mode_inv, sweep_inv):
    table = jnp.asarray(cas_tables())
    up, down = pl.pallas_call(
        functools.partial(pack_rows, FIRST),
        in_specs=[VMEM] * 3,
        out_specs=[VMEM] * 2,
        out_shape=[shape(len(FIRST), LINES, 4, NZ)] * 2,
        compiler_params=params(60),
        name="pack_first",
    )(vel, rhs_mom, sweep_inv)
    low, high = both_ways(up, down, "radial", False)
    fwd = pl.pallas_call(
        pack_forward,
        grid=(1,),
        in_specs=[pl.BlockSpec((3, 4, CR, NZ), lambda i: (0, 1, 0, 0))] * 2
        + [pl.BlockSpec((3, 3, 4, CR, NZ), lambda i: (0, 0, 1, 0, 0))],
        out_specs=pl.BlockSpec((48, CR, NZ), lambda i: (0, 0, 0)),
        out_shape=shape(48, CR, NZ),
        compiler_params=params(60),
        name="pack_forward",
    )(vel, rhs_mom, sweep_inv)
    fwd, low, high = lax.optimization_barrier((fwd, low, high))
    before = lax.ppermute(fwd, "pitch", [(i, (i + 1) % BLOCKS) for i in range(BLOCKS)])
    sent = pl.pallas_call(
        div_kernel,
        grid=(1,),
        in_specs=[pl.BlockSpec((3, LINES, CR, NZ), lambda i: (0, 0, 0, 0))]
        + [pl.BlockSpec((1, LINES, 4, NZ), lambda i: (FIRST.index(13), 0, 0, 0))] * 2,
        out_specs=pl.BlockSpec((NZ, 128), lambda i: (0, 0)),
        out_shape=shape(NZ, 128),
        compiler_params=params(60),
        name="divergence",
    )(vel, low, high)
    sent = sent.reshape(BLOCKS, CHUNK, 128)
    vel_b, rhs_b, inv_b, sent = lax.optimization_barrier((vel, rhs_mom, sweep_inv, sent))
    got = lax.all_to_all(sent, "pitch", split_axis=0, concat_axis=0, tiled=True)
    bwd, up, down = pl.pallas_call(
        pack_rest,
        in_specs=[VMEM] * 3,
        out_specs=[VMEM] * 3,
        out_shape=[shape(48, CR, NZ)] + [shape(len(BULK), LINES, 4, NZ)] * 2,
        compiler_params=params(60),
        name="pack_rest",
    )(vel_b, rhs_b, inv_b)
    after = lax.ppermute(bwd, "pitch", [((i + 1) % BLOCKS, i) for i in range(BLOCKS)])

    bef = corners(0, before)
    got, bef = lax.optimization_barrier((got, bef))
    modes = jnp.transpose(mode_inv, (1, 2, 0))
    sent = pl.pallas_call(
        modes_kernel,
        in_specs=[VMEM] * 3,
        out_specs=VMEM,
        out_shape=shape(NZ, 128),
        compiler_params=params(8),
        name="modes",
    )(got.reshape(NZ, 128), modes, table)
    sent = sent.reshape(BLOCKS, CHUNK, 128)
    got = lax.all_to_all(sent, "pitch", split_axis=0, concat_axis=0, tiled=True)
    up, down, _ = lax.optimization_barrier((up, down, sent))
    after, _ = lax.optimization_barrier((after, sent))
    rad_low, rad_high = both_ways(up, down, "radial", False)
    aft = corners(1, after)
    press, up, down = pl.pallas_call(
        turn_kernel,
        in_specs=[VMEM] * 5,
        out_specs=[VMEM] * 3,
        out_shape=[shape(128, NZ)] + [shape(26, CR, NZ)] * 2,
        compiler_params=params(8),
        name="turn",
    )(got.reshape(NZ, 128), *bef, *aft)
    cor_low, cor_high = both_ways(up, down, "radial", False)

    return pl.pallas_call(
        sweep_kernel,
        in_specs=[VMEM] * 12,
        out_specs=[VMEM] * 2,
        out_shape=[shape(3, LINES, CR, NZ), shape(LINES, CR, NZ)],
        scratch_shapes=[
            pltpu.VMEM((9, 14, 16, NZ), F32),
            pltpu.VMEM((3, 14, 16, NZ), F32),
            pltpu.VMEM((2, 3, 16, 16, NZ), F32),
            pltpu.VMEM((16, 16, NZ), F32),
        ],
        compiler_params=params(16),
        name="sweeps",
    )(vel, rhs_mom, sweep_inv, press, before, after, low, high, rad_low, rad_high, cor_low, cor_high)


def solution(mesh):
    return jax.shard_map(
        on_device,
        mesh=mesh,
        in_specs=(
            P(None, "pitch", "radial", None),
            P(None, "pitch", "radial", None),
            P(None, "radial", None),
            P(None, None, "pitch", "radial", None),
        ),
        out_specs=(P(None, "pitch", "radial", None), P("pitch", "radial", None)),
        check_vma=False,
    )
```

```python
import functools

import jax
import jax.numpy as jnp
import ml_dtypes
import numpy as np
from jax import lax
from jax.experimental import pallas as pl
from jax.experimental.pallas import tpu as pltpu
from jax.sharding import PartitionSpec as P

SWEEPS = 4
BULK = tuple(range(13)) + (14,)
coupling = 0.5
NP, CR, NZ = 512, 8, 256
BLOCKS = 64
LINES = NP // BLOCKS
CHUNK = NZ // BLOCKS
F32 = jnp.float32
BF16 = jnp.bfloat16


def cas_tables():
    index = np.arange(NP)
    angle = 2.0 * np.pi / NP * (index[:, None] * index[None, :] % NP)
    table = np.cos(angle) + np.sin(angle)
    order = (np.arange(BLOCKS)[None, :] * LINES + np.arange(LINES)[:, None]).reshape(-1)
    mat = table[order, :]
    high = mat.astype(ml_dtypes.bfloat16)
    low = (mat - high.astype(np.float64)).astype(ml_dtypes.bfloat16)
    return np.concatenate([high, low])


def params(mib=24):
    return pltpu.CompilerParams(vmem_limit_bytes=mib * 1024 * 1024)


VMEM = pl.BlockSpec(memory_space=pltpu.VMEM)


def shape(*dims):
    return jax.ShapeDtypeStruct(dims, F32)


def axial(x, step):
    lane = lax.broadcasted_iota(jnp.int32, x.shape, x.ndim - 1)
    moved = pltpu.roll(x, (-step) % NZ, x.ndim - 1)
    return jnp.where(lane == (NZ - 1 if step > 0 else 0), 0.0, moved)


def pack_first(v1, up, down):
    up[0] = v1[0, :, 4:8, :]
    down[0] = v1[0, :, 0:4, :]


def pack_rows(vel, rhs, inv, up, down):
    for n, f in enumerate(BULK):
        src = inv.at[f // 3, f % 3] if f < 9 else rhs.at[f - 9] if f < 12 else vel.at[f - 12]
        up[n] = src[:, 4:8, :]
        down[n] = src[:, 0:4, :]


def div_kernel(vel, low, high, out):
    row = lax.broadcasted_iota(jnp.int32, (CR, NZ), 0)
    parts = []
    for l in range(LINES):
        v1, v2 = vel[1, l], vel[2, l]
        upper = jnp.where(row == CR - 1, high[0, l, 0:1, :], pltpu.roll(v1, CR - 1, 0))
        lower = jnp.where(row == 0, low[0, l, 3:4, :], pltpu.roll(v1, 1, 0))
        parts.append(((upper - lower) + (axial(v2, 1) - axial(v2, -1))) * 0.5)
    for l in range(LINES):
        parts.append(vel[0, l])
    out[...] = jnp.concatenate(parts, axis=0).T


def block_shift(x, step):
    lane = lax.broadcasted_iota(jnp.int32, x.shape, 1) % BLOCKS
    edge = BLOCKS - 1 if step > 0 else 0
    near = pltpu.roll(x, (-step) % 128, 1)
    far = pltpu.roll(x, (BLOCKS - step) % 128, 1)
    return jnp.where(lane == edge, far, near)


def split_dot(x, table, dim):
    dims = (((1,), (dim,)), ((), ()))
    xh = x.astype(BF16)
    xl = (x - xh.astype(F32)).astype(BF16)
    rows = x.shape[0]
    both = jnp.concatenate([xh, xl], axis=0)
    both = lax.dot_general(both, table[0:NP], dims, preferred_element_type=F32)
    cross = lax.dot_general(xh, table[NP : 2 * NP], dims, preferred_element_type=F32)
    return both[:rows] + (both[rows:] + cross)


def modes_kernel(got, mode, table, out):
    lane = lax.broadcasted_iota(jnp.int32, (CR, 128), 1)
    sub = lax.broadcasted_iota(jnp.int32, (CR, 128), 0)
    left = lane < BLOCKS
    half = CHUNK // 2
    rows = [[None] * 4 for _ in range(CHUNK)]
    for pair in range(half):
        slabs = [got[pl.ds(2 * pair + e, BLOCKS, stride=CHUNK), :] for e in range(2)]
        a = jnp.concatenate(slabs, axis=0).T
        w = [a[l * CR : (l + 1) * CR] for l in range(LINES)]
        v = [a[NP // 8 + l * CR : NP // 8 + (l + 1) * CR] for l in range(LINES)]
        before = [block_shift(v[-1], -1)] + v[:-1]
        after = v[1:] + [block_shift(v[0], 1)]
        d = [w[l] + (after[l] - before[l]) * 0.5 for l in range(LINES)]
        for t in range(4):
            e, o = d[2 * t], d[2 * t + 1]
            rows[2 * pair][t] = jnp.where(left, e, pltpu.roll(o, BLOCKS, 1))
            rows[2 * pair + 1][t] = jnp.where(left, pltpu.roll(e, BLOCKS, 1), o)
    x = jnp.concatenate([jnp.concatenate(r, axis=1) for r in rows], axis=0)
    dhat = split_dot(x, table, 0)
    q = []
    for z in range(CHUNK):
        total = None
        for s in range(CR):
            term = mode[:, s, :] * dhat[z * CR + s : z * CR + s + 1, :]
            total = term if total is None else total + term
        q.append(total)
    p = split_dot(jnp.concatenate(q, axis=0), table, 1) * (1.0 / NP)
    for pair in range(half):
        e = []
        for t in range(4):
            a = p[2 * pair * CR : (2 * pair + 1) * CR, t * 128 : (t + 1) * 128]
            b = p[(2 * pair + 1) * CR : (2 * pair + 2) * CR, t * 128 : (t + 1) * 128]
            e.append(jnp.where(left, a, pltpu.roll(b, BLOCKS, 1)))
            e.append(jnp.where(left, pltpu.roll(a, BLOCKS, 1), b))
        wide = [block_shift(x, -1) for x in e[4:]] + e + [block_shift(x, 1) for x in e[:4]]
        low, high = [], []
        for m in range(8):
            a, b = wide[2 * m], wide[2 * m + 1]
            low.append(jnp.where(sub < 4, a, pltpu.roll(b, 4, 0)))
            high.append(jnp.where(sub < 4, pltpu.roll(a, 4, 0), b))
        turned = jnp.concatenate(low + high, axis=0).T
        for z in range(2):
            out[pl.ds(2 * pair + z, BLOCKS, stride=CHUNK), :] = turned[
                z * BLOCKS : (z + 1) * BLOCKS
            ]


def pack_forward(vel, rhs, inv, fwd):
    for f in range(9):
        fwd[3 * f : 3 * f + 3] = inv[f // 3, f % 3, 1:4]
    for c in range(3):
        fwd[27 + 3 * c : 30 + 3 * c] = rhs[c, 1:4]
        fwd[36 + 4 * c : 40 + 4 * c] = vel[c]


def pack_rest(vel, rhs, inv, bwd, up, down):
    for f in range(9):
        bwd[3 * f : 3 * f + 3] = inv[f // 3, f % 3, 0:3]
    for c in range(3):
        bwd[27 + 3 * c : 30 + 3 * c] = rhs[c, 0:3]
        bwd[36 + 4 * c : 40 + 4 * c] = vel[c, 0:4]
    pack_rows(vel, rhs, inv, up, down)


def corner_kernel(side, halo, up, down):
    for out, first in ((up, 4), (down, 0)):
        two = first + 2 if first else 0
        for f in range(12):
            for n in range(2):
                src = halo[3 * f + n + 1 - side]
                out[f // 2, 4 * (f % 2) + 2 * n : 4 * (f % 2) + 2 * n + 2, :] = src[two : two + 2]
        for c in range(3):
            g = 36 + 4 * c
            out[6 + c, 0:4, :] = halo[g + 3 - 3 * side, first : first + 4, :]
            for n in range(2):
                src = halo[g + 1 + n]
                out[6 + c, 4 + 2 * n : 6 + 2 * n, :] = src[two : two + 2]


def turn_kernel(got, bef_up, bef_down, aft_up, aft_down, press, up, down):
    turned = got[...].T
    press[...] = turned
    for m in range(8):
        up[m] = turned[64 + 8 * m : 72 + 8 * m]
        down[m] = turned[8 * m : 8 * m + 8]
    up[8:17] = bef_up[...]
    down[8:17] = bef_down[...]
    up[17:26] = aft_up[...]
    down[17:26] = aft_down[...]


def beyond(f, first, bulk):
    return bulk[BULK.index(f)] if f in BULK else first[0]


def sweep_kernel(vel, rhs, inv, press, before, after, low, high, rad_low, rad_high, cor_low, cor_high,
                 velocity, pressure, es, ef, eu, ep):
    for l in range(16):
        ep[l, 4:8, :] = press[4 * l : 4 * l + 4]
        ep[l, 8:12, :] = press[64 + 4 * l : 68 + 4 * l]
        ep[l, 0:4, :] = cor_low[l // 2, 4 * (l % 2) : 4 * (l % 2) + 4, :]
        ep[l, 12:16, :] = cor_high[l // 2, 4 * (l % 2) : 4 * (l % 2) + 4, :]
    for l in range(LINES):
        pressure[l] = ep[l + 4, 4:12, :]
    for f in range(12):
        c, d = f // 3, f % 3
        dst = es.at[f] if f < 9 else ef.at[f - 9]
        own = inv.at[c, d] if f < 9 else rhs.at[f - 9]
        dst[3:11, 4:12, :] = own[...]
        dst[3:11, 0:4, :] = beyond(f, low, rad_low)
        dst[3:11, 12:16, :] = beyond(f, high, rad_high)
        dst[0:3, 4:12, :] = before[3 * f : 3 * f + 3]
        dst[11:14, 4:12, :] = after[3 * f : 3 * f + 3]
        for n, line in enumerate((1, 2, 11, 12)):
            t, r = 8 + 9 * (n // 2) + f // 2, 4 * (f % 2) + 2 * (n % 2)
            dst[line, 2:4, :] = cor_low[t, r : r + 2, :]
            dst[line, 12:14, :] = cor_high[t, r : r + 2, :]
    for c in range(3):
        dst = eu.at[0, c]
        g = 36 + 4 * c
        dst[4:12, 4:12, :] = vel[c]
        dst[4:12, 0:4, :] = beyond(12 + c, low, rad_low)
        dst[4:12, 12:16, :] = beyond(12 + c, high, rad_high)
        dst[0:4, 4:12, :] = before[g : g + 4]
        dst[12:16, 4:12, :] = after[g : g + 4]
        for n, line in enumerate((3, 12)):
            t = 14 + 9 * n + c
            dst[line, 0:4, :] = cor_low[t, 0:4, :]
            dst[line, 12:16, :] = cor_high[t, 0:4, :]
        for n, line in enumerate((1, 2, 13, 14)):
            t, r = 14 + 9 * (n // 2) + c, 4 + 2 * (n % 2)
            dst[line, 2:4, :] = cor_low[t, r : r + 2, :]
            dst[line, 12:14, :] = cor_high[t, r : r + 2, :]

    def line_step(sweep, j):
        now, later = sweep % 2, 1 - sweep % 2
        if sweep == 0:
            mid = ep[j + 1]
            ef[0, j] = ef[0, j] - (ep[j + 2] - ep[j]) * 0.5
            ef[1, j] = ef[1, j] - (pltpu.roll(mid, 15, 0) - pltpu.roll(mid, 1, 0)) * 0.5
            ef[2, j] = ef[2, j] - (axial(mid, 1) - axial(mid, -1)) * 0.5
        state, res = [], []
        for c in range(3):
            u = eu[now, c, j + 1]
            beside = (eu[now, c, j] + eu[now, c, j + 2]) + (pltpu.roll(u, 15, 0) + pltpu.roll(u, 1, 0))
            beside = beside + (axial(u, 1) + axial(u, -1))
            state.append(u)
            res.append(ef[c, j] - ((1.0 + 6.0 * coupling) * u - coupling * beside))
        for c in range(3):
            new = state[c] + es[3 * c, j] * res[0] + es[3 * c + 1, j] * res[1] + es[3 * c + 2, j] * res[2]
            if sweep == SWEEPS - 1:
                velocity[c, j - 3] = new[4:12]
            else:
                eu[later, c, j + 1] = new

    for sweep in range(SWEEPS):
        for j in range(sweep, 14 - sweep):
            line_step(sweep, j)


def both_ways(up, down, axis, periodic):
    count = lax.axis_size(axis)
    forward = [(i, i + 1) for i in range(count - 1)]
    if periodic:
        forward.append((count - 1, 0))
    backward = [(target, source) for source, target in forward]
    return lax.ppermute(up, axis, forward), lax.ppermute(down, axis, backward)


def corners(side, halo):
    return pl.pallas_call(
        functools.partial(corner_kernel, side),
        in_specs=[VMEM],
        out_specs=[VMEM] * 2,
        out_shape=[shape(9, CR, NZ)] * 2,
        compiler_params=params(8),
        name="corners",
    )(halo)


def on_device(vel, rhs_mom, mode_inv, sweep_inv):
    table = jnp.asarray(cas_tables())
    up, down = pl.pallas_call(
        pack_first,
        grid=(1,),
        in_specs=[pl.BlockSpec((1, LINES, CR, NZ), lambda i: (1, 0, 0, 0))],
        out_specs=[pl.BlockSpec((1, LINES, 4, NZ), lambda i: (0, 0, 0, 0))] * 2,
        out_shape=[shape(1, LINES, 4, NZ)] * 2,
        compiler_params=params(60),
        name="pack_first",
    )(vel)
    low, high = both_ways(up, down, "radial", False)
    fwd = pl.pallas_call(
        pack_forward,
        grid=(1,),
        in_specs=[pl.BlockSpec((3, 4, CR, NZ), lambda i: (0, 1, 0, 0))] * 2
        + [pl.BlockSpec((3, 3, 4, CR, NZ), lambda i: (0, 0, 1, 0, 0))],
        out_specs=pl.BlockSpec((48, CR, NZ), lambda i: (0, 0, 0)),
        out_shape=shape(48, CR, NZ),
        compiler_params=params(60),
        name="pack_forward",
    )(vel, rhs_mom, sweep_inv)
    fwd, low, high = lax.optimization_barrier((fwd, low, high))
    before = lax.ppermute(fwd, "pitch", [(i, (i + 1) % BLOCKS) for i in range(BLOCKS)])
    sent = pl.pallas_call(
        div_kernel,
        grid=(1,),
        in_specs=[pl.BlockSpec((3, LINES, CR, NZ), lambda i: (0, 0, 0, 0))]
        + [pl.BlockSpec((1, LINES, 4, NZ), lambda i: (0, 0, 0, 0))] * 2,
        out_specs=pl.BlockSpec((NZ, 128), lambda i: (0, 0)),
        out_shape=shape(NZ, 128),
        compiler_params=params(60),
        name="divergence",
    )(vel, low, high)
    sent = sent.reshape(BLOCKS, CHUNK, 128)
    vel_b, rhs_b, inv_b, sent = lax.optimization_barrier((vel, rhs_mom, sweep_inv, sent))
    got = lax.all_to_all(sent, "pitch", split_axis=0, concat_axis=0, tiled=True)
    bwd, up, down = pl.pallas_call(
        pack_rest,
        in_specs=[VMEM] * 3,
        out_specs=[VMEM] * 3,
        out_shape=[shape(48, CR, NZ)] + [shape(len(BULK), LINES, 4, NZ)] * 2,
        compiler_params=params(60),
        name="pack_rest",
    )(vel_b, rhs_b, inv_b)
    after = lax.ppermute(bwd, "pitch", [((i + 1) % BLOCKS, i) for i in range(BLOCKS)])

    bef = corners(0, before)
    got, bef = lax.optimization_barrier((got, bef))
    modes = jnp.transpose(mode_inv, (1, 2, 0))
    sent = pl.pallas_call(
        modes_kernel,
        in_specs=[VMEM] * 3,
        out_specs=VMEM,
        out_shape=shape(NZ, 128),
        compiler_params=params(8),
        name="modes",
    )(got.reshape(NZ, 128), modes, table)
    sent = sent.reshape(BLOCKS, CHUNK, 128)
    got = lax.all_to_all(sent, "pitch", split_axis=0, concat_axis=0, tiled=True)
    up, down, _ = lax.optimization_barrier((up, down, sent))
    after, _ = lax.optimization_barrier((after, sent))
    rad_low, rad_high = both_ways(up, down, "radial", False)
    aft = corners(1, after)
    press, up, down = pl.pallas_call(
        turn_kernel,
        in_specs=[VMEM] * 5,
        out_specs=[VMEM] * 3,
        out_shape=[shape(128, NZ)] + [shape(26, CR, NZ)] * 2,
        compiler_params=params(8),
        name="turn",
    )(got.reshape(NZ, 128), *bef, *aft)
    cor_low, cor_high = both_ways(up, down, "radial", False)

    return pl.pallas_call(
        sweep_kernel,
        in_specs=[VMEM] * 12,
        out_specs=[VMEM] * 2,
        out_shape=[shape(3, LINES, CR, NZ), shape(LINES, CR, NZ)],
        scratch_shapes=[
            pltpu.VMEM((9, 14, 16, NZ), F32),
            pltpu.VMEM((3, 14, 16, NZ), F32),
            pltpu.VMEM((2, 3, 16, 16, NZ), F32),
            pltpu.VMEM((16, 16, NZ), F32),
        ],
        compiler_params=params(16),
        name="sweeps",
    )(vel, rhs_mom, sweep_inv, press, before, after, low, high, rad_low, rad_high, cor_low, cor_high)


def solution(mesh):
    return jax.shard_map(
        on_device,
        mesh=mesh,
        in_specs=(
            P(None, "pitch", "radial", None),
            P(None, "pitch", "radial", None),
            P(None, "radial", None),
            P(None, None, "pitch", "radial", None),
        ),
        out_specs=(P(None, "pitch", "radial", None), P("pitch", "radial", None)),
        check_vma=False,
    )
```

```python
import functools

import jax
import jax.numpy as jnp
import ml_dtypes
import numpy as np
from jax import lax
from jax.experimental import pallas as pl
from jax.experimental.pallas import tpu as pltpu
from jax.sharding import PartitionSpec as P

SWEEPS = 4
BULK = tuple(range(13)) + (14,)
coupling = 0.5
NP, CR, NZ = 512, 8, 256
BLOCKS = 64
LINES = NP // BLOCKS
CHUNK = NZ // BLOCKS
F32 = jnp.float32
BF16 = jnp.bfloat16


def cas_tables():
    index = np.arange(NP)
    angle = 2.0 * np.pi / NP * (index[:, None] * index[None, :] % NP)
    table = np.cos(angle) + np.sin(angle)
    order = (np.arange(BLOCKS)[None, :] * LINES + np.arange(LINES)[:, None]).reshape(-1)
    mat = table[order, :]
    high = mat.astype(ml_dtypes.bfloat16)
    low = (mat - high.astype(np.float64)).astype(ml_dtypes.bfloat16)
    return np.concatenate([high, low])


def params(mib=24):
    return pltpu.CompilerParams(vmem_limit_bytes=mib * 1024 * 1024)


VMEM = pl.BlockSpec(memory_space=pltpu.VMEM)


def shape(*dims):
    return jax.ShapeDtypeStruct(dims, F32)


def axial(x, step):
    lane = lax.broadcasted_iota(jnp.int32, x.shape, x.ndim - 1)
    moved = pltpu.roll(x, (-step) % NZ, x.ndim - 1)
    return jnp.where(lane == (NZ - 1 if step > 0 else 0), 0.0, moved)


def pack_first(v1, up, down):
    up[0] = v1[0, :, 4:8, :]
    down[0] = v1[0, :, 0:4, :]


def pack_rows(vel, rhs, inv, up, down):
    for n, f in enumerate(BULK):
        src = inv.at[f // 3, f % 3] if f < 9 else rhs.at[f - 9] if f < 12 else vel.at[f - 12]
        up[n] = src[:, 4:8, :]
        down[n] = src[:, 0:4, :]


def div_kernel(vel, low, high, out):
    row = lax.broadcasted_iota(jnp.int32, (CR, NZ), 0)
    parts = []
    for l in range(LINES):
        v1, v2 = vel[1, l], vel[2, l]
        upper = jnp.where(row == CR - 1, high[0, l, 0:1, :], pltpu.roll(v1, CR - 1, 0))
        lower = jnp.where(row == 0, low[0, l, 3:4, :], pltpu.roll(v1, 1, 0))
        parts.append(((upper - lower) + (axial(v2, 1) - axial(v2, -1))) * 0.5)
    for l in range(LINES):
        parts.append(vel[0, l])
    out[...] = jnp.concatenate(parts, axis=0).T


def block_shift(x, step):
    lane = lax.broadcasted_iota(jnp.int32, x.shape, 1) % BLOCKS
    edge = BLOCKS - 1 if step > 0 else 0
    near = pltpu.roll(x, (-step) % 128, 1)
    far = pltpu.roll(x, (BLOCKS - step) % 128, 1)
    return jnp.where(lane == edge, far, near)


def split_dot(x, table, dim):
    dims = (((1,), (dim,)), ((), ()))
    xh = x.astype(BF16)
    xl = (x - xh.astype(F32)).astype(BF16)
    rows = x.shape[0]
    both = jnp.concatenate([xh, xl], axis=0)
    both = lax.dot_general(both, table[0:NP], dims, preferred_element_type=F32)
    cross = lax.dot_general(xh, table[NP : 2 * NP], dims, preferred_element_type=F32)
    return both[:rows] + (both[rows:] + cross)


def modes_kernel(got, mode, table, out):
    lane = lax.broadcasted_iota(jnp.int32, (CR, 128), 1)
    sub = lax.broadcasted_iota(jnp.int32, (CR, 128), 0)
    left = lane < BLOCKS
    half = CHUNK // 2
    rows = [[None] * 4 for _ in range(CHUNK)]
    for pair in range(half):
        slabs = [got[pl.ds(2 * pair + e, BLOCKS, stride=CHUNK), :] for e in range(2)]
        a = jnp.concatenate(slabs, axis=0).T
        w = [a[l * CR : (l + 1) * CR] for l in range(LINES)]
        v = [a[NP // 8 + l * CR : NP // 8 + (l + 1) * CR] for l in range(LINES)]
        before = [block_shift(v[-1], -1)] + v[:-1]
        after = v[1:] + [block_shift(v[0], 1)]
        d = [w[l] + (after[l] - before[l]) * 0.5 for l in range(LINES)]
        for t in range(4):
            e, o = d[2 * t], d[2 * t + 1]
            rows[2 * pair][t] = jnp.where(left, e, pltpu.roll(o, BLOCKS, 1))
            rows[2 * pair + 1][t] = jnp.where(left, pltpu.roll(e, BLOCKS, 1), o)
    x = jnp.concatenate([jnp.concatenate(r, axis=1) for r in rows], axis=0)
    dhat = split_dot(x, table, 0)
    q = []
    for z in range(CHUNK):
        total = None
        for s in range(CR):
            term = mode[:, s, :] * dhat[z * CR + s : z * CR + s + 1, :]
            total = term if total is None else total + term
        q.append(total)
    p = split_dot(jnp.concatenate(q, axis=0), table, 1) * (1.0 / NP)
    for pair in range(half):
        e = []
        for t in range(4):
            a = p[2 * pair * CR : (2 * pair + 1) * CR, t * 128 : (t + 1) * 128]
            b = p[(2 * pair + 1) * CR : (2 * pair + 2) * CR, t * 128 : (t + 1) * 128]
            e.append(jnp.where(left, a, pltpu.roll(b, BLOCKS, 1)))
            e.append(jnp.where(left, pltpu.roll(a, BLOCKS, 1), b))
        wide = [block_shift(x, -1) for x in e[4:]] + e + [block_shift(x, 1) for x in e[:4]]
        low, high = [], []
        for m in range(8):
            a, b = wide[2 * m], wide[2 * m + 1]
            low.append(jnp.where(sub < 4, a, pltpu.roll(b, 4, 0)))
            high.append(jnp.where(sub < 4, pltpu.roll(a, 4, 0), b))
        turned = jnp.concatenate(low + high, axis=0).T
        for z in range(2):
            out[pl.ds(2 * pair + z, BLOCKS, stride=CHUNK), :] = turned[
                z * BLOCKS : (z + 1) * BLOCKS
            ]


def pack_forward(vel, rhs, inv, fwd):
    for f in range(9):
        fwd[3 * f : 3 * f + 3] = inv[f // 3, f % 3, 1:4]
    for c in range(3):
        fwd[27 + 3 * c] = rhs[c, 1] + coupling * vel[c, 0]
        fwd[28 + 3 * c : 30 + 3 * c] = rhs[c, 2:4]
        fwd[36 + 3 * c : 39 + 3 * c] = vel[c, 1:4]


def pack_rest(vel, rhs, inv, bwd, up, down):
    for f in range(9):
        bwd[3 * f : 3 * f + 3] = inv[f // 3, f % 3, 0:3]
    for c in range(3):
        bwd[27 + 3 * c : 29 + 3 * c] = rhs[c, 0:2]
        bwd[29 + 3 * c] = rhs[c, 2] + coupling * vel[c, 3]
        bwd[36 + 3 * c : 39 + 3 * c] = vel[c, 0:3]
    pack_rows(vel, rhs, inv, up, down)


def corner_kernel(side, halo, up, down):
    for out, first in ((up, 4), (down, 0)):
        two = first + 2 if first else 0
        for f in range(12):
            for n in range(2):
                src = halo[3 * f + n + 1 - side]
                out[f // 2, 4 * (f % 2) + 2 * n : 4 * (f % 2) + 2 * n + 2, :] = src[two : two + 2]
        for c in range(3):
            g = 36 + 3 * c
            out[6 + c, 0:4, :] = halo[g + 2 - 2 * side, first : first + 4, :]
            for n in range(2):
                src = halo[g + n + side]
                out[6 + c, 4 + 2 * n : 6 + 2 * n, :] = src[two : two + 2]


def turn_kernel(got, bef_up, bef_down, aft_up, aft_down, press, up, down):
    turned = got[...].T
    press[...] = turned
    for m in range(8):
        up[m] = turned[64 + 8 * m : 72 + 8 * m]
        down[m] = turned[8 * m : 8 * m + 8]
    up[8:17] = bef_up[...]
    down[8:17] = bef_down[...]
    up[17:26] = aft_up[...]
    down[17:26] = aft_down[...]


def beyond(f, first, bulk):
    return bulk[BULK.index(f)] if f in BULK else first[0]


def sweep_kernel(vel, rhs, inv, press, before, after, low, high, rad_low, rad_high, cor_low, cor_high,
                 velocity, pressure, es, ef, eu, ep):
    for l in range(16):
        ep[l, 4:8, :] = press[4 * l : 4 * l + 4]
        ep[l, 8:12, :] = press[64 + 4 * l : 68 + 4 * l]
        ep[l, 0:4, :] = cor_low[l // 2, 4 * (l % 2) : 4 * (l % 2) + 4, :]
        ep[l, 12:16, :] = cor_high[l // 2, 4 * (l % 2) : 4 * (l % 2) + 4, :]
    for l in range(LINES):
        pressure[l] = ep[l + 4, 4:12, :]
    for f in range(12):
        c, d = f // 3, f % 3
        dst = es.at[f] if f < 9 else ef.at[f - 9]
        own = inv.at[c, d] if f < 9 else rhs.at[f - 9]
        dst[3:11, 4:12, :] = own[...]
        dst[3:11, 0:4, :] = beyond(f, low, rad_low)
        dst[3:11, 12:16, :] = beyond(f, high, rad_high)
        dst[0:3, 4:12, :] = before[3 * f : 3 * f + 3]
        dst[11:14, 4:12, :] = after[3 * f : 3 * f + 3]
        for n, line in enumerate((1, 2, 11, 12)):
            t, r = 8 + 9 * (n // 2) + f // 2, 4 * (f % 2) + 2 * (n % 2)
            dst[line, 2:4, :] = cor_low[t, r : r + 2, :]
            dst[line, 12:14, :] = cor_high[t, r : r + 2, :]
    for c in range(3):
        dst = eu.at[0, c]
        g = 36 + 3 * c
        dst[4:12, 4:12, :] = vel[c]
        dst[4:12, 0:4, :] = beyond(12 + c, low, rad_low)
        dst[4:12, 12:16, :] = beyond(12 + c, high, rad_high)
        dst[1:4, 4:12, :] = before[g : g + 3]
        dst[12:15, 4:12, :] = after[g : g + 3]
        dst[0, 4:12, :] = dst[15, 4:12, :] = jnp.zeros((CR, NZ), F32)
        for n, line in enumerate((3, 12)):
            t = 14 + 9 * n + c
            dst[line, 0:4, :] = cor_low[t, 0:4, :]
            dst[line, 12:16, :] = cor_high[t, 0:4, :]
        for n, line in enumerate((1, 2, 13, 14)):
            t, r = 14 + 9 * (n // 2) + c, 4 + 2 * (n % 2)
            dst[line, 2:4, :] = cor_low[t, r : r + 2, :]
            dst[line, 12:14, :] = cor_high[t, r : r + 2, :]

    def line_step(sweep, j):
        now, later = sweep % 2, 1 - sweep % 2
        if sweep == 0:
            mid = ep[j + 1]
            ef[0, j] = ef[0, j] - (ep[j + 2] - ep[j]) * 0.5
            ef[1, j] = ef[1, j] - (pltpu.roll(mid, 15, 0) - pltpu.roll(mid, 1, 0)) * 0.5
            ef[2, j] = ef[2, j] - (axial(mid, 1) - axial(mid, -1)) * 0.5
        state, res = [], []
        for c in range(3):
            u = eu[now, c, j + 1]
            beside = (eu[now, c, j] + eu[now, c, j + 2]) + (pltpu.roll(u, 15, 0) + pltpu.roll(u, 1, 0))
            beside = beside + (axial(u, 1) + axial(u, -1))
            state.append(u)
            res.append(ef[c, j] - ((1.0 + 6.0 * coupling) * u - coupling * beside))
        for c in range(3):
            new = state[c] + es[3 * c, j] * res[0] + es[3 * c + 1, j] * res[1] + es[3 * c + 2, j] * res[2]
            if sweep == SWEEPS - 1:
                velocity[c, j - 3] = new[4:12]
            else:
                eu[later, c, j + 1] = new

    for sweep in range(SWEEPS):
        for j in range(sweep, 14 - sweep):
            line_step(sweep, j)


def both_ways(up, down, axis, periodic):
    count = lax.axis_size(axis)
    forward = [(i, i + 1) for i in range(count - 1)]
    if periodic:
        forward.append((count - 1, 0))
    backward = [(target, source) for source, target in forward]
    return lax.ppermute(up, axis, forward), lax.ppermute(down, axis, backward)


def corners(side, halo):
    return pl.pallas_call(
        functools.partial(corner_kernel, side),
        in_specs=[VMEM],
        out_specs=[VMEM] * 2,
        out_shape=[shape(9, CR, NZ)] * 2,
        compiler_params=params(8),
        name="corners",
    )(halo)


def on_device(vel, rhs_mom, mode_inv, sweep_inv):
    table = jnp.asarray(cas_tables())
    up, down = pl.pallas_call(
        pack_first,
        grid=(1,),
        in_specs=[pl.BlockSpec((1, LINES, CR, NZ), lambda i: (1, 0, 0, 0))],
        out_specs=[pl.BlockSpec((1, LINES, 4, NZ), lambda i: (0, 0, 0, 0))] * 2,
        out_shape=[shape(1, LINES, 4, NZ)] * 2,
        compiler_params=params(60),
        name="pack_first",
    )(vel)
    low, high = both_ways(up, down, "radial", False)
    fwd = pl.pallas_call(
        pack_forward,
        grid=(1,),
        in_specs=[pl.BlockSpec((3, 4, CR, NZ), lambda i: (0, 1, 0, 0))] * 2
        + [pl.BlockSpec((3, 3, 4, CR, NZ), lambda i: (0, 0, 1, 0, 0))],
        out_specs=pl.BlockSpec((45, CR, NZ), lambda i: (0, 0, 0)),
        out_shape=shape(45, CR, NZ),
        compiler_params=params(60),
        name="pack_forward",
    )(vel, rhs_mom, sweep_inv)
    fwd, low, high = lax.optimization_barrier((fwd, low, high))
    before = lax.ppermute(fwd, "pitch", [(i, (i + 1) % BLOCKS) for i in range(BLOCKS)])
    sent = pl.pallas_call(
        div_kernel,
        grid=(1,),
        in_specs=[pl.BlockSpec((3, LINES, CR, NZ), lambda i: (0, 0, 0, 0))]
        + [pl.BlockSpec((1, LINES, 4, NZ), lambda i: (0, 0, 0, 0))] * 2,
        out_specs=pl.BlockSpec((NZ, 128), lambda i: (0, 0)),
        out_shape=shape(NZ, 128),
        compiler_params=params(60),
        name="divergence",
    )(vel, low, high)
    sent = sent.reshape(BLOCKS, CHUNK, 128)
    vel_b, rhs_b, inv_b, sent = lax.optimization_barrier((vel, rhs_mom, sweep_inv, sent))
    got = lax.all_to_all(sent, "pitch", split_axis=0, concat_axis=0, tiled=True)
    bwd, up, down = pl.pallas_call(
        pack_rest,
        in_specs=[VMEM] * 3,
        out_specs=[VMEM] * 3,
        out_shape=[shape(45, CR, NZ)] + [shape(len(BULK), LINES, 4, NZ)] * 2,
        compiler_params=params(60),
        name="pack_rest",
    )(vel_b, rhs_b, inv_b)
    after = lax.ppermute(bwd, "pitch", [((i + 1) % BLOCKS, i) for i in range(BLOCKS)])

    bef = corners(0, before)
    got, bef = lax.optimization_barrier((got, bef))
    modes = jnp.transpose(mode_inv, (1, 2, 0))
    sent = pl.pallas_call(
        modes_kernel,
        in_specs=[VMEM] * 3,
        out_specs=VMEM,
        out_shape=shape(NZ, 128),
        compiler_params=params(8),
        name="modes",
    )(got.reshape(NZ, 128), modes, table)
    sent = sent.reshape(BLOCKS, CHUNK, 128)
    got = lax.all_to_all(sent, "pitch", split_axis=0, concat_axis=0, tiled=True)
    up, down, _ = lax.optimization_barrier((up, down, sent))
    after, _ = lax.optimization_barrier((after, sent))
    rad_low, rad_high = both_ways(up, down, "radial", False)
    aft = corners(1, after)
    press, up, down = pl.pallas_call(
        turn_kernel,
        in_specs=[VMEM] * 5,
        out_specs=[VMEM] * 3,
        out_shape=[shape(128, NZ)] + [shape(26, CR, NZ)] * 2,
        compiler_params=params(8),
        name="turn",
    )(got.reshape(NZ, 128), *bef, *aft)
    cor_low, cor_high = both_ways(up, down, "radial", False)

    return pl.pallas_call(
        sweep_kernel,
        in_specs=[VMEM] * 12,
        out_specs=[VMEM] * 2,
        out_shape=[shape(3, LINES, CR, NZ), shape(LINES, CR, NZ)],
        scratch_shapes=[
            pltpu.VMEM((9, 14, 16, NZ), F32),
            pltpu.VMEM((3, 14, 16, NZ), F32),
            pltpu.VMEM((2, 3, 16, 16, NZ), F32),
            pltpu.VMEM((16, 16, NZ), F32),
        ],
        compiler_params=params(16),
        name="sweeps",
    )(vel, rhs_mom, sweep_inv, press, before, after, low, high, rad_low, rad_high, cor_low, cor_high)


def solution(mesh):
    return jax.shard_map(
        on_device,
        mesh=mesh,
        in_specs=(
            P(None, "pitch", "radial", None),
            P(None, "pitch", "radial", None),
            P(None, "radial", None),
            P(None, None, "pitch", "radial", None),
        ),
        out_specs=(P(None, "pitch", "radial", None), P("pitch", "radial", None)),
        check_vma=False,
    )
```

```python
import functools

import jax
import jax.numpy as jnp
import ml_dtypes
import numpy as np
from jax import lax
from jax.experimental import pallas as pl
from jax.experimental.pallas import tpu as pltpu
from jax.sharding import PartitionSpec as P

SWEEPS = 4
BULK = tuple(range(13)) + (14,)
coupling = 0.5
NP, CR, NZ = 512, 8, 256
BLOCKS = 64
LINES = NP // BLOCKS
CHUNK = NZ // BLOCKS
F32 = jnp.float32
BF16 = jnp.bfloat16


def cas_tables():
    index = np.arange(NP)
    angle = 2.0 * np.pi / NP * (index[:, None] * index[None, :] % NP)
    table = np.cos(angle) + np.sin(angle)
    order = (np.arange(BLOCKS)[None, :] * LINES + np.arange(LINES)[:, None]).reshape(-1)
    mat = table[order, :]
    high = mat.astype(ml_dtypes.bfloat16)
    low = (mat - high.astype(np.float64)).astype(ml_dtypes.bfloat16)
    return np.concatenate([high, low])


def params(mib=24):
    return pltpu.CompilerParams(vmem_limit_bytes=mib * 1024 * 1024)


VMEM = pl.BlockSpec(memory_space=pltpu.VMEM)


def shape(*dims):
    return jax.ShapeDtypeStruct(dims, F32)


def axial(x, step):
    lane = lax.broadcasted_iota(jnp.int32, x.shape, x.ndim - 1)
    moved = pltpu.roll(x, (-step) % NZ, x.ndim - 1)
    return jnp.where(lane == (NZ - 1 if step > 0 else 0), 0.0, moved)


def pack_first(v1, up, down):
    up[0] = v1[0, :, 4:8, :]
    down[0] = v1[0, :, 0:4, :]


def pack_rows(vel, rhs, inv, up, down):
    for n, f in enumerate(BULK):
        src = inv.at[f // 3, f % 3] if f < 9 else rhs.at[f - 9] if f < 12 else vel.at[f - 12]
        up[n] = src[:, 4:8, :]
        down[n] = src[:, 0:4, :]


def div_kernel(vel, low, high, out):
    row = lax.broadcasted_iota(jnp.int32, (CR, NZ), 0)
    parts = []
    for l in range(LINES):
        v1, v2 = vel[1, l], vel[2, l]
        upper = jnp.where(row == CR - 1, high[0, l, 0:1, :], pltpu.roll(v1, CR - 1, 0))
        lower = jnp.where(row == 0, low[0, l, 3:4, :], pltpu.roll(v1, 1, 0))
        parts.append(((upper - lower) + (axial(v2, 1) - axial(v2, -1))) * 0.5)
    for l in range(LINES):
        parts.append(vel[0, l])
    out[...] = jnp.concatenate(parts, axis=0).T


def block_shift(x, step):
    lane = lax.broadcasted_iota(jnp.int32, x.shape, 1) % BLOCKS
    edge = BLOCKS - 1 if step > 0 else 0
    near = pltpu.roll(x, (-step) % 128, 1)
    far = pltpu.roll(x, (BLOCKS - step) % 128, 1)
    return jnp.where(lane == edge, far, near)


def split_dot(x, table, dim):
    dims = (((1,), (dim,)), ((), ()))
    xh = x.astype(BF16)
    xl = (x - xh.astype(F32)).astype(BF16)
    rows = x.shape[0]
    both = jnp.concatenate([xh, xl], axis=0)
    both = lax.dot_general(both, table[0:NP], dims, preferred_element_type=F32)
    cross = lax.dot_general(xh, table[NP : 2 * NP], dims, preferred_element_type=F32)
    return both[:rows] + (both[rows:] + cross)


def modes_kernel(got, mode, table, out):
    lane = lax.broadcasted_iota(jnp.int32, (CR, 128), 1)
    sub = lax.broadcasted_iota(jnp.int32, (CR, 128), 0)
    left = lane < BLOCKS
    half = CHUNK // 2
    rows = [[None] * 4 for _ in range(CHUNK)]
    for pair in range(half):
        slabs = [got[pl.ds(2 * pair + e, BLOCKS, stride=CHUNK), :] for e in range(2)]
        a = jnp.concatenate(slabs, axis=0).T
        w = [a[l * CR : (l + 1) * CR] for l in range(LINES)]
        v = [a[NP // 8 + l * CR : NP // 8 + (l + 1) * CR] for l in range(LINES)]
        before = [block_shift(v[-1], -1)] + v[:-1]
        after = v[1:] + [block_shift(v[0], 1)]
        d = [w[l] + (after[l] - before[l]) * 0.5 for l in range(LINES)]
        for t in range(4):
            e, o = d[2 * t], d[2 * t + 1]
            rows[2 * pair][t] = jnp.where(left, e, pltpu.roll(o, BLOCKS, 1))
            rows[2 * pair + 1][t] = jnp.where(left, pltpu.roll(e, BLOCKS, 1), o)
    x = jnp.concatenate([jnp.concatenate(r, axis=1) for r in rows], axis=0)
    dhat = split_dot(x, table, 0)
    q = []
    for z in range(CHUNK):
        total = None
        for s in range(CR):
            term = mode[:, s, :] * dhat[z * CR + s : z * CR + s + 1, :]
            total = term if total is None else total + term
        q.append(total)
    p = split_dot(jnp.concatenate(q, axis=0), table, 1) * (1.0 / NP)
    for pair in range(half):
        e = []
        for t in range(4):
            a = p[2 * pair * CR : (2 * pair + 1) * CR, t * 128 : (t + 1) * 128]
            b = p[(2 * pair + 1) * CR : (2 * pair + 2) * CR, t * 128 : (t + 1) * 128]
            e.append(jnp.where(left, a, pltpu.roll(b, BLOCKS, 1)))
            e.append(jnp.where(left, pltpu.roll(a, BLOCKS, 1), b))
        wide = [block_shift(x, -1) for x in e[4:]] + e + [block_shift(x, 1) for x in e[:4]]
        low, high = [], []
        for m in range(8):
            a, b = wide[2 * m], wide[2 * m + 1]
            low.append(jnp.where(sub < 4, a, pltpu.roll(b, 4, 0)))
            high.append(jnp.where(sub < 4, pltpu.roll(a, 4, 0), b))
        turned = jnp.concatenate(low + high, axis=0).T
        for z in range(2):
            out[pl.ds(2 * pair + z, BLOCKS, stride=CHUNK), :] = turned[
                z * BLOCKS : (z + 1) * BLOCKS
            ]


def pack_forward(vel, rhs, inv, fwd):
    for f in range(9):
        fwd[3 * f : 3 * f + 3] = inv[f // 3, f % 3, 1:4]
    for c in range(3):
        fwd[27 + 3 * c] = rhs[c, 1] + coupling * vel[c, 0]
        fwd[28 + 3 * c : 30 + 3 * c] = rhs[c, 2:4]
        fwd[36 + 3 * c : 39 + 3 * c] = vel[c, 1:4]


def pack_rest(vel, rhs, inv, bwd, up, down):
    for f in range(9):
        bwd[3 * f : 3 * f + 3] = inv[f // 3, f % 3, 0:3]
    for c in range(3):
        bwd[27 + 3 * c : 29 + 3 * c] = rhs[c, 0:2]
        bwd[29 + 3 * c] = rhs[c, 2] + coupling * vel[c, 3]
        bwd[36 + 3 * c : 39 + 3 * c] = vel[c, 0:3]
    pack_rows(vel, rhs, inv, up, down)


def corner_kernel(side, halo, up, down):
    for out, first in ((up, 4), (down, 0)):
        two = first + 2 if first else 0
        for f in range(12):
            for n in range(2):
                src = halo[3 * f + n + 1 - side]
                out[f // 2, 4 * (f % 2) + 2 * n : 4 * (f % 2) + 2 * n + 2, :] = src[two : two + 2]
        for c in range(3):
            g = 36 + 3 * c
            out[6 + c, 0:4, :] = halo[g + 2 - 2 * side, first : first + 4, :]
            for n in range(2):
                src = halo[g + n + side]
                out[6 + c, 4 + 2 * n : 6 + 2 * n, :] = src[two : two + 2]


def turn_kernel(got, bef_up, bef_down, aft_up, aft_down, press, up, down):
    turned = got[...].T
    press[...] = turned
    for m in range(8):
        up[m] = turned[64 + 8 * m : 72 + 8 * m]
        down[m] = turned[8 * m : 8 * m + 8]
    up[8:17] = bef_up[...]
    down[8:17] = bef_down[...]
    up[17:26] = aft_up[...]
    down[17:26] = aft_down[...]


def beyond(f, first, bulk):
    return bulk[BULK.index(f)] if f in BULK else first[0]


def sweep_kernel(vel, rhs, inv, press, before, after, low, high, rad_low, rad_high, cor_low, cor_high,
                 velocity, pressure, es, ef, eu, ep):
    for l in range(16):
        ep[l, 4:8, :] = press[4 * l : 4 * l + 4]
        ep[l, 8:12, :] = press[64 + 4 * l : 68 + 4 * l]
        ep[l, 0:4, :] = cor_low[l // 2, 4 * (l % 2) : 4 * (l % 2) + 4, :]
        ep[l, 12:16, :] = cor_high[l // 2, 4 * (l % 2) : 4 * (l % 2) + 4, :]
    for l in range(LINES):
        pressure[l] = ep[l + 4, 4:12, :]
    for f in range(12):
        c, d = f // 3, f % 3
        dst = es.at[f] if f < 9 else ef.at[f - 9]
        own = inv.at[c, d] if f < 9 else rhs.at[f - 9]
        dst[3:11, 4:12, :] = own[...]
        dst[3:11, 0:4, :] = beyond(f, low, rad_low)
        dst[3:11, 12:16, :] = beyond(f, high, rad_high)
        dst[0:3, 4:12, :] = before[3 * f : 3 * f + 3]
        dst[11:14, 4:12, :] = after[3 * f : 3 * f + 3]
        for n, line in enumerate((1, 2, 11, 12)):
            t, r = 8 + 9 * (n // 2) + f // 2, 4 * (f % 2) + 2 * (n % 2)
            dst[line, 2:4, :] = cor_low[t, r : r + 2, :]
            dst[line, 12:14, :] = cor_high[t, r : r + 2, :]
    for c in range(3):
        dst = eu.at[0, c]
        g = 36 + 3 * c
        dst[4:12, 4:12, :] = vel[c]
        dst[4:12, 0:4, :] = beyond(12 + c, low, rad_low)
        dst[4:12, 12:16, :] = beyond(12 + c, high, rad_high)
        dst[1:4, 4:12, :] = before[g : g + 3]
        dst[12:15, 4:12, :] = after[g : g + 3]
        dst[0, 4:12, :] = dst[15, 4:12, :] = jnp.zeros((CR, NZ), F32)
        for n, line in enumerate((3, 12)):
            t = 14 + 9 * n + c
            dst[line, 0:4, :] = cor_low[t, 0:4, :]
            dst[line, 12:16, :] = cor_high[t, 0:4, :]
        for n, line in enumerate((1, 2, 13, 14)):
            t, r = 14 + 9 * (n // 2) + c, 4 + 2 * (n % 2)
            dst[line, 2:4, :] = cor_low[t, r : r + 2, :]
            dst[line, 12:14, :] = cor_high[t, r : r + 2, :]

    def line_step(sweep, j):
        now, later = sweep % 2, 1 - sweep % 2
        if sweep == 0:
            mid = ep[j + 1]
            ef[0, j] = ef[0, j] - (ep[j + 2] - ep[j]) * 0.5
            ef[1, j] = ef[1, j] - (pltpu.roll(mid, 15, 0) - pltpu.roll(mid, 1, 0)) * 0.5
            ef[2, j] = ef[2, j] - (axial(mid, 1) - axial(mid, -1)) * 0.5
        state, res = [], []
        for c in range(3):
            u = eu[now, c, j + 1]
            beside = (eu[now, c, j] + eu[now, c, j + 2]) + (pltpu.roll(u, 15, 0) + pltpu.roll(u, 1, 0))
            beside = beside + (axial(u, 1) + axial(u, -1))
            state.append(u)
            res.append(ef[c, j] - ((1.0 + 6.0 * coupling) * u - coupling * beside))
        for c in range(3):
            new = state[c] + es[3 * c, j] * res[0] + es[3 * c + 1, j] * res[1] + es[3 * c + 2, j] * res[2]
            if sweep == SWEEPS - 1:
                velocity[c, j - 3] = new[4:12]
            else:
                eu[later, c, j + 1] = new

    for sweep in range(SWEEPS):
        for j in range(sweep, 14 - sweep):
            line_step(sweep, j)


def both_ways(up, down, axis, periodic):
    count = lax.axis_size(axis)
    forward = [(i, i + 1) for i in range(count - 1)]
    if periodic:
        forward.append((count - 1, 0))
    backward = [(target, source) for source, target in forward]
    return lax.ppermute(up, axis, forward), lax.ppermute(down, axis, backward)


def corners(side, halo):
    return pl.pallas_call(
        functools.partial(corner_kernel, side),
        in_specs=[VMEM],
        out_specs=[VMEM] * 2,
        out_shape=[shape(9, CR, NZ)] * 2,
        compiler_params=params(8),
        name="corners",
    )(halo)


def on_device(vel, rhs_mom, mode_inv, sweep_inv):
    table = jnp.asarray(cas_tables())
    up, down = pl.pallas_call(
        pack_first,
        grid=(1,),
        in_specs=[pl.BlockSpec((1, LINES, CR, NZ), lambda i: (1, 0, 0, 0))],
        out_specs=[pl.BlockSpec((1, LINES, 4, NZ), lambda i: (0, 0, 0, 0))] * 2,
        out_shape=[shape(1, LINES, 4, NZ)] * 2,
        compiler_params=params(24),
        name="pack_first",
    )(vel)
    low, high = both_ways(up, down, "radial", False)
    fwd = pl.pallas_call(
        pack_forward,
        grid=(1,),
        in_specs=[pl.BlockSpec((3, 4, CR, NZ), lambda i: (0, 1, 0, 0))] * 2
        + [pl.BlockSpec((3, 3, 4, CR, NZ), lambda i: (0, 0, 1, 0, 0))],
        out_specs=pl.BlockSpec((45, CR, NZ), lambda i: (0, 0, 0)),
        out_shape=shape(45, CR, NZ),
        compiler_params=params(60),
        name="pack_forward",
    )(vel, rhs_mom, sweep_inv)
    fwd, low, high = lax.optimization_barrier((fwd, low, high))
    before = lax.ppermute(fwd, "pitch", [(i, (i + 1) % BLOCKS) for i in range(BLOCKS)])
    sent = pl.pallas_call(
        div_kernel,
        grid=(1,),
        in_specs=[pl.BlockSpec((3, LINES, CR, NZ), lambda i: (0, 0, 0, 0))]
        + [pl.BlockSpec((1, LINES, 4, NZ), lambda i: (0, 0, 0, 0))] * 2,
        out_specs=pl.BlockSpec((NZ, 128), lambda i: (0, 0)),
        out_shape=shape(NZ, 128),
        compiler_params=params(24),
        name="divergence",
    )(vel, low, high)
    sent = sent.reshape(BLOCKS, CHUNK, 128)
    vel_b, rhs_b, inv_b, sent = lax.optimization_barrier((vel, rhs_mom, sweep_inv, sent))
    got = lax.all_to_all(sent, "pitch", split_axis=0, concat_axis=0, tiled=True)
    bwd, up, down = pl.pallas_call(
        pack_rest,
        in_specs=[VMEM] * 3,
        out_specs=[VMEM] * 3,
        out_shape=[shape(45, CR, NZ)] + [shape(len(BULK), LINES, 4, NZ)] * 2,
        compiler_params=params(60),
        name="pack_rest",
    )(vel_b, rhs_b, inv_b)
    after = lax.ppermute(bwd, "pitch", [((i + 1) % BLOCKS, i) for i in range(BLOCKS)])

    bef = corners(0, before)
    got, bef = lax.optimization_barrier((got, bef))
    modes = jnp.transpose(mode_inv, (1, 2, 0))
    sent = pl.pallas_call(
        modes_kernel,
        in_specs=[VMEM] * 3,
        out_specs=VMEM,
        out_shape=shape(NZ, 128),
        compiler_params=params(8),
        name="modes",
    )(got.reshape(NZ, 128), modes, table)
    sent = sent.reshape(BLOCKS, CHUNK, 128)
    got = lax.all_to_all(sent, "pitch", split_axis=0, concat_axis=0, tiled=True)
    up, down, _ = lax.optimization_barrier((up, down, sent))
    after, _ = lax.optimization_barrier((after, sent))
    rad_low, rad_high = both_ways(up, down, "radial", False)
    aft = corners(1, after)
    press, up, down = pl.pallas_call(
        turn_kernel,
        in_specs=[VMEM] * 5,
        out_specs=[VMEM] * 3,
        out_shape=[shape(128, NZ)] + [shape(26, CR, NZ)] * 2,
        compiler_params=params(8),
        name="turn",
    )(got.reshape(NZ, 128), *bef, *aft)
    cor_low, cor_high = both_ways(up, down, "radial", False)

    return pl.pallas_call(
        sweep_kernel,
        in_specs=[VMEM] * 12,
        out_specs=[VMEM] * 2,
        out_shape=[shape(3, LINES, CR, NZ), shape(LINES, CR, NZ)],
        scratch_shapes=[
            pltpu.VMEM((9, 14, 16, NZ), F32),
            pltpu.VMEM((3, 14, 16, NZ), F32),
            pltpu.VMEM((2, 3, 16, 16, NZ), F32),
            pltpu.VMEM((16, 16, NZ), F32),
        ],
        compiler_params=params(16),
        name="sweeps",
    )(vel, rhs_mom, sweep_inv, press, before, after, low, high, rad_low, rad_high, cor_low, cor_high)


def solution(mesh):
    return jax.shard_map(
        on_device,
        mesh=mesh,
        in_specs=(
            P(None, "pitch", "radial", None),
            P(None, "pitch", "radial", None),
            P(None, "radial", None),
            P(None, None, "pitch", "radial", None),
        ),
        out_specs=(P(None, "pitch", "radial", None), P("pitch", "radial", None)),
        check_vma=False,
    )
```

```python
import functools

import jax
import jax.numpy as jnp
import ml_dtypes
import numpy as np
from jax import lax
from jax.experimental import pallas as pl
from jax.experimental.pallas import tpu as pltpu
from jax.sharding import PartitionSpec as P

SWEEPS = 4
BULK = tuple(range(13)) + (14,)
coupling = 0.5
NP, CR, NZ = 512, 8, 256
BLOCKS = 64
LINES = NP // BLOCKS
CHUNK = NZ // BLOCKS
F32 = jnp.float32
BF16 = jnp.bfloat16


def cas_tables():
    index = np.arange(NP)
    angle = 2.0 * np.pi / NP * (index[:, None] * index[None, :] % NP)
    table = np.cos(angle) + np.sin(angle)
    order = (np.arange(BLOCKS)[None, :] * LINES + np.arange(LINES)[:, None]).reshape(-1)
    mat = table[order, :]
    high = mat.astype(ml_dtypes.bfloat16)
    low = (mat - high.astype(np.float64)).astype(ml_dtypes.bfloat16)
    return np.concatenate([high, low])


def params(mib=24):
    return pltpu.CompilerParams(vmem_limit_bytes=mib * 1024 * 1024)


VMEM = pl.BlockSpec(memory_space=pltpu.VMEM)


def shape(*dims):
    return jax.ShapeDtypeStruct(dims, F32)


def axial(x, step):
    lane = lax.broadcasted_iota(jnp.int32, x.shape, x.ndim - 1)
    moved = pltpu.roll(x, (-step) % NZ, x.ndim - 1)
    return jnp.where(lane == (NZ - 1 if step > 0 else 0), 0.0, moved)


def pack_first(v1, up, down):
    up[0] = v1[0, :, 4:8, :]
    down[0] = v1[0, :, 0:4, :]


def pack_rows(vel, rhs, inv, up, down):
    for n, f in enumerate(BULK):
        src = inv.at[f // 3, f % 3] if f < 9 else rhs.at[f - 9] if f < 12 else vel.at[f - 12]
        up[n] = src[:, 4:8, :]
        down[n] = src[:, 0:4, :]


def div_kernel(vel, low, high, out):
    row = lax.broadcasted_iota(jnp.int32, (CR, NZ), 0)
    parts = []
    for l in range(LINES):
        v1, v2 = vel[1, l], vel[2, l]
        upper = jnp.where(row == CR - 1, high[0, l, 0:1, :], pltpu.roll(v1, CR - 1, 0))
        lower = jnp.where(row == 0, low[0, l, 3:4, :], pltpu.roll(v1, 1, 0))
        parts.append(((upper - lower) + (axial(v2, 1) - axial(v2, -1))) * 0.5)
    for l in range(LINES):
        parts.append(vel[0, l])
    out[...] = jnp.concatenate(parts, axis=0).T


def block_shift(x, step):
    lane = lax.broadcasted_iota(jnp.int32, x.shape, 1) % BLOCKS
    edge = BLOCKS - 1 if step > 0 else 0
    near = pltpu.roll(x, (-step) % 128, 1)
    far = pltpu.roll(x, (BLOCKS - step) % 128, 1)
    return jnp.where(lane == edge, far, near)


def split_dot(x, table, dim):
    dims = (((1,), (dim,)), ((), ()))
    xh = x.astype(BF16)
    xl = (x - xh.astype(F32)).astype(BF16)
    rows = x.shape[0]
    both = jnp.concatenate([xh, xl], axis=0)
    both = lax.dot_general(both, table[0:NP], dims, preferred_element_type=F32)
    cross = lax.dot_general(xh, table[NP : 2 * NP], dims, preferred_element_type=F32)
    return both[:rows] + (both[rows:] + cross)


def modes_kernel(got, mode, table, out):
    lane = lax.broadcasted_iota(jnp.int32, (CR, 128), 1)
    sub = lax.broadcasted_iota(jnp.int32, (CR, 128), 0)
    left = lane < BLOCKS
    half = CHUNK // 2
    rows = [[None] * 4 for _ in range(CHUNK)]
    for pair in range(half):
        slabs = [got[pl.ds(2 * pair + e, BLOCKS, stride=CHUNK), :] for e in range(2)]
        a = jnp.concatenate(slabs, axis=0).T
        w = [a[l * CR : (l + 1) * CR] for l in range(LINES)]
        v = [a[NP // 8 + l * CR : NP // 8 + (l + 1) * CR] for l in range(LINES)]
        before = [block_shift(v[-1], -1)] + v[:-1]
        after = v[1:] + [block_shift(v[0], 1)]
        d = [w[l] + (after[l] - before[l]) * 0.5 for l in range(LINES)]
        for t in range(4):
            e, o = d[2 * t], d[2 * t + 1]
            rows[2 * pair][t] = jnp.where(left, e, pltpu.roll(o, BLOCKS, 1))
            rows[2 * pair + 1][t] = jnp.where(left, pltpu.roll(e, BLOCKS, 1), o)
    x = jnp.concatenate([jnp.concatenate(r, axis=1) for r in rows], axis=0)
    dhat = split_dot(x, table, 0)
    q = []
    for z in range(CHUNK):
        total = None
        for s in range(CR):
            term = mode[:, s, :] * dhat[z * CR + s : z * CR + s + 1, :]
            total = term if total is None else total + term
        q.append(total)
    p = split_dot(jnp.concatenate(q, axis=0), table, 1) * (1.0 / NP)
    for pair in range(half):
        e = []
        for t in range(4):
            a = p[2 * pair * CR : (2 * pair + 1) * CR, t * 128 : (t + 1) * 128]
            b = p[(2 * pair + 1) * CR : (2 * pair + 2) * CR, t * 128 : (t + 1) * 128]
            e.append(jnp.where(left, a, pltpu.roll(b, BLOCKS, 1)))
            e.append(jnp.where(left, pltpu.roll(a, BLOCKS, 1), b))
        wide = [block_shift(x, -1) for x in e[4:]] + e + [block_shift(x, 1) for x in e[:4]]
        low, high = [], []
        for m in range(8):
            a, b = wide[2 * m], wide[2 * m + 1]
            low.append(jnp.where(sub < 4, a, pltpu.roll(b, 4, 0)))
            high.append(jnp.where(sub < 4, pltpu.roll(a, 4, 0), b))
        turned = jnp.concatenate(low + high, axis=0).T
        for z in range(2):
            out[pl.ds(2 * pair + z, BLOCKS, stride=CHUNK), :] = turned[
                z * BLOCKS : (z + 1) * BLOCKS
            ]


def pack_forward(vel, rhs, inv, fwd):
    for f in range(9):
        fwd[3 * f : 3 * f + 3] = inv[f // 3, f % 3, 1:4]
    for c in range(3):
        fwd[27 + 3 * c] = rhs[c, 1] + coupling * vel[c, 0]
        fwd[28 + 3 * c : 30 + 3 * c] = rhs[c, 2:4]
        fwd[36 + 3 * c : 39 + 3 * c] = vel[c, 1:4]


def pack_rest(vel, rhs, inv, bwd, up, down):
    for f in range(9):
        bwd[3 * f : 3 * f + 3] = inv[f // 3, f % 3, 0:3]
    for c in range(3):
        bwd[27 + 3 * c : 29 + 3 * c] = rhs[c, 0:2]
        bwd[29 + 3 * c] = rhs[c, 2] + coupling * vel[c, 3]
        bwd[36 + 3 * c : 39 + 3 * c] = vel[c, 0:3]
    pack_rows(vel, rhs, inv, up, down)


def corner_kernel(side, halo, up, down):
    for out, first in ((up, 4), (down, 0)):
        two = first + 2 if first else 0
        for f in range(12):
            for n in range(2):
                src = halo[3 * f + n + 1 - side]
                out[f // 2, 4 * (f % 2) + 2 * n : 4 * (f % 2) + 2 * n + 2, :] = src[two : two + 2]
        for c in range(3):
            g = 36 + 3 * c
            out[6 + c, 0:4, :] = halo[g + 2 - 2 * side, first : first + 4, :]
            for n in range(2):
                src = halo[g + n + side]
                out[6 + c, 4 + 2 * n : 6 + 2 * n, :] = src[two : two + 2]


def turn_kernel(got, bef_up, bef_down, aft_up, aft_down, press, up, down):
    turned = got[...].T
    press[...] = turned
    for m in range(8):
        up[m] = turned[64 + 8 * m : 72 + 8 * m]
        down[m] = turned[8 * m : 8 * m + 8]
    up[8:17] = bef_up[...]
    down[8:17] = bef_down[...]
    up[17:26] = aft_up[...]
    down[17:26] = aft_down[...]


def beyond(f, first, bulk):
    return bulk[BULK.index(f)] if f in BULK else first[0]


def sweep_kernel(vel, rhs, inv, press, before, after, low, high, rad_low, rad_high, cor_low, cor_high,
                 velocity, pressure, es, ef, eu, ep):
    for l in range(16):
        ep[l, 4:8, :] = press[4 * l : 4 * l + 4]
        ep[l, 8:12, :] = press[64 + 4 * l : 68 + 4 * l]
        ep[l, 0:4, :] = cor_low[l // 2, 4 * (l % 2) : 4 * (l % 2) + 4, :]
        ep[l, 12:16, :] = cor_high[l // 2, 4 * (l % 2) : 4 * (l % 2) + 4, :]
    for l in range(LINES):
        pressure[l] = ep[l + 4, 4:12, :]
    for f in range(12):
        c, d = f // 3, f % 3
        dst = es.at[f] if f < 9 else ef.at[f - 9]
        own = inv.at[c, d] if f < 9 else rhs.at[f - 9]
        dst[3:11, 4:12, :] = own[...]
        dst[3:11, 0:4, :] = beyond(f, low, rad_low)
        dst[3:11, 12:16, :] = beyond(f, high, rad_high)
        dst[0:3, 4:12, :] = before[3 * f : 3 * f + 3]
        dst[11:14, 4:12, :] = after[3 * f : 3 * f + 3]
        for n, line in enumerate((1, 2, 11, 12)):
            t, r = 8 + 9 * (n // 2) + f // 2, 4 * (f % 2) + 2 * (n % 2)
            dst[line, 2:4, :] = cor_low[t, r : r + 2, :]
            dst[line, 12:14, :] = cor_high[t, r : r + 2, :]
    for c in range(3):
        dst = eu.at[0, c]
        g = 36 + 3 * c
        dst[4:12, 4:12, :] = vel[c]
        dst[4:12, 0:4, :] = beyond(12 + c, low, rad_low)
        dst[4:12, 12:16, :] = beyond(12 + c, high, rad_high)
        dst[1:4, 4:12, :] = before[g : g + 3]
        dst[12:15, 4:12, :] = after[g : g + 3]
        dst[0, 4:12, :] = dst[15, 4:12, :] = jnp.zeros((CR, NZ), F32)
        for n, line in enumerate((3, 12)):
            t = 14 + 9 * n + c
            dst[line, 0:4, :] = cor_low[t, 0:4, :]
            dst[line, 12:16, :] = cor_high[t, 0:4, :]
        for n, line in enumerate((1, 2, 13, 14)):
            t, r = 14 + 9 * (n // 2) + c, 4 + 2 * (n % 2)
            dst[line, 2:4, :] = cor_low[t, r : r + 2, :]
            dst[line, 12:14, :] = cor_high[t, r : r + 2, :]

    def line_step(sweep, j):
        now, later = sweep % 2, 1 - sweep % 2
        if sweep == 0:
            mid = ep[j + 1]
            ef[0, j] = ef[0, j] - (ep[j + 2] - ep[j]) * 0.5
            ef[1, j] = ef[1, j] - (pltpu.roll(mid, 15, 0) - pltpu.roll(mid, 1, 0)) * 0.5
            ef[2, j] = ef[2, j] - (axial(mid, 1) - axial(mid, -1)) * 0.5
        state, res = [], []
        for c in range(3):
            u = eu[now, c, j + 1]
            beside = (eu[now, c, j] + eu[now, c, j + 2]) + (pltpu.roll(u, 15, 0) + pltpu.roll(u, 1, 0))
            beside = beside + (axial(u, 1) + axial(u, -1))
            state.append(u)
            res.append(ef[c, j] - ((1.0 + 6.0 * coupling) * u - coupling * beside))
        for c in range(3):
            new = state[c] + es[3 * c, j] * res[0] + es[3 * c + 1, j] * res[1] + es[3 * c + 2, j] * res[2]
            if sweep == SWEEPS - 1:
                velocity[c, j - 3] = new[4:12]
            else:
                eu[later, c, j + 1] = new

    for sweep in range(SWEEPS):
        for j in range(sweep, 14 - sweep):
            line_step(sweep, j)


def both_ways(up, down, axis, periodic):
    count = lax.axis_size(axis)
    forward = [(i, i + 1) for i in range(count - 1)]
    if periodic:
        forward.append((count - 1, 0))
    backward = [(target, source) for source, target in forward]
    return lax.ppermute(up, axis, forward), lax.ppermute(down, axis, backward)


def corners(side, halo):
    return pl.pallas_call(
        functools.partial(corner_kernel, side),
        in_specs=[VMEM],
        out_specs=[VMEM] * 2,
        out_shape=[shape(9, CR, NZ)] * 2,
        compiler_params=params(8),
        name="corners",
    )(halo)


def on_device(vel, rhs_mom, mode_inv, sweep_inv):
    table = jnp.asarray(cas_tables())
    up, down = pl.pallas_call(
        pack_first,
        grid=(1,),
        in_specs=[pl.BlockSpec((1, LINES, CR, NZ), lambda i: (1, 0, 0, 0))],
        out_specs=[pl.BlockSpec((1, LINES, 4, NZ), lambda i: (0, 0, 0, 0))] * 2,
        out_shape=[shape(1, LINES, 4, NZ)] * 2,
        compiler_params=params(24),
        name="pack_first",
    )(vel)
    low, high = both_ways(up, down, "radial", False)
    fwd = pl.pallas_call(
        pack_forward,
        grid=(1,),
        in_specs=[pl.BlockSpec((3, 4, CR, NZ), lambda i: (0, 1, 0, 0))] * 2
        + [pl.BlockSpec((3, 3, 4, CR, NZ), lambda i: (0, 0, 1, 0, 0))],
        out_specs=pl.BlockSpec((45, CR, NZ), lambda i: (0, 0, 0)),
        out_shape=shape(45, CR, NZ),
        compiler_params=params(24),
        name="pack_forward",
    )(vel, rhs_mom, sweep_inv)
    fwd, low, high = lax.optimization_barrier((fwd, low, high))
    before = lax.ppermute(fwd, "pitch", [(i, (i + 1) % BLOCKS) for i in range(BLOCKS)])
    sent = pl.pallas_call(
        div_kernel,
        grid=(1,),
        in_specs=[pl.BlockSpec((3, LINES, CR, NZ), lambda i: (0, 0, 0, 0))]
        + [pl.BlockSpec((1, LINES, 4, NZ), lambda i: (0, 0, 0, 0))] * 2,
        out_specs=pl.BlockSpec((NZ, 128), lambda i: (0, 0)),
        out_shape=shape(NZ, 128),
        compiler_params=params(24),
        name="divergence",
    )(vel, low, high)
    sent = sent.reshape(BLOCKS, CHUNK, 128)
    vel_b, rhs_b, inv_b, sent = lax.optimization_barrier((vel, rhs_mom, sweep_inv, sent))
    got = lax.all_to_all(sent, "pitch", split_axis=0, concat_axis=0, tiled=True)
    bwd, up, down = pl.pallas_call(
        pack_rest,
        in_specs=[VMEM] * 3,
        out_specs=[VMEM] * 3,
        out_shape=[shape(45, CR, NZ)] + [shape(len(BULK), LINES, 4, NZ)] * 2,
        compiler_params=params(60),
        name="pack_rest",
    )(vel_b, rhs_b, inv_b)
    after = lax.ppermute(bwd, "pitch", [((i + 1) % BLOCKS, i) for i in range(BLOCKS)])

    bef = corners(0, before)
    got, bef = lax.optimization_barrier((got, bef))
    modes = jnp.transpose(mode_inv, (1, 2, 0))
    sent = pl.pallas_call(
        modes_kernel,
        in_specs=[VMEM] * 3,
        out_specs=VMEM,
        out_shape=shape(NZ, 128),
        compiler_params=params(8),
        name="modes",
    )(got.reshape(NZ, 128), modes, table)
    sent = sent.reshape(BLOCKS, CHUNK, 128)
    got = lax.all_to_all(sent, "pitch", split_axis=0, concat_axis=0, tiled=True)
    up, down, _ = lax.optimization_barrier((up, down, sent))
    after, _ = lax.optimization_barrier((after, sent))
    rad_low, rad_high = both_ways(up, down, "radial", False)
    aft = corners(1, after)
    press, up, down = pl.pallas_call(
        turn_kernel,
        in_specs=[VMEM] * 5,
        out_specs=[VMEM] * 3,
        out_shape=[shape(128, NZ)] + [shape(26, CR, NZ)] * 2,
        compiler_params=params(8),
        name="turn",
    )(got.reshape(NZ, 128), *bef, *aft)
    cor_low, cor_high = both_ways(up, down, "radial", False)

    return pl.pallas_call(
        sweep_kernel,
        in_specs=[VMEM] * 12,
        out_specs=[VMEM] * 2,
        out_shape=[shape(3, LINES, CR, NZ), shape(LINES, CR, NZ)],
        scratch_shapes=[
            pltpu.VMEM((9, 14, 16, NZ), F32),
            pltpu.VMEM((3, 14, 16, NZ), F32),
            pltpu.VMEM((2, 3, 16, 16, NZ), F32),
            pltpu.VMEM((16, 16, NZ), F32),
        ],
        compiler_params=params(16),
        name="sweeps",
    )(vel, rhs_mom, sweep_inv, press, before, after, low, high, rad_low, rad_high, cor_low, cor_high)


def solution(mesh):
    return jax.shard_map(
        on_device,
        mesh=mesh,
        in_specs=(
            P(None, "pitch", "radial", None),
            P(None, "pitch", "radial", None),
            P(None, "radial", None),
            P(None, None, "pitch", "radial", None),
        ),
        out_specs=(P(None, "pitch", "radial", None), P("pitch", "radial", None)),
        check_vma=False,
    )
```
